256 devices in a mesh: ta: 2 (over y_lo), gx: 128 (over y_hi, z, x, core).
Axes of the slice: x: 4, y: 4 (y_hi: 2, y_lo: 2; y = y_hi * 2 + y_lo), z: 8, core: 2. Of those that a mesh axis runs over, the one named last changes fastest.
Arguments:
- modes: bfloat16 [12, 96, 131072], P('ta', None, 'gx'), parts along dimension 0, may hold values from -6 to 6
- links: float32 [6, 18, 131072], P('ta', None, 'gx'), parts along dimension 0, may hold values from -2.5 to 2.5
- sites: int32 [6144], P(('ta', 'gx')), parts along dimension 0, may hold values from 0 to 1023, as said below
- counts: int32 [256], P(('ta', 'gx')), parts along dimension 0, may hold values from 1 to 24, as said below
- pair_table: int32 [9216], P('gx'), may hold values from 0 to 9215, each once
Outputs:
- elementals: float32 [18432, 192], P(('ta', 'gx')), parts along dimension 0
The draws below stay inside these ranges and needn't reach their ends.
There are 2 independent parts, one for each index of `ta`. The reference program is written for one: setup_inputs(seed, part) draws one part's arguments, and reference() takes and returns one part's arrays. A program takes and returns all parts, laid end to end along the dimension named above; an argument that names none is the same for every part. Nothing has to cross between parts.
Inputs may be any that keep to these rules, and one draw needn't show every extreme that they name: `counts`: some device has all 24 slots live. `sites`: the first slot of every device lists a site in that device's last x-plane.
All inputs are finite; a program needn't handle non-finite values.
Results may differ from the reference program's by a relative error of at most 0.0057.
Values may be sent and summed in bfloat16 or wider, within the bound.
No kernel may reach another device: no remote copies, remote signals or barrier semaphores. Data moves between devices by JAX's collectives and lax.ppermute only.
A program may use at most 128 MiB of HBM per device.

```python
import jax
import jax.numpy as jnp
from jax import lax

MODES = 96
LX = 4
LY = 16
LZ = 16
SLOTS = 24
NSITES = 131072
NLIST = 3072
NPAIRS = 9216


def draw_counts(key, part):
    key = jax.random.fold_in(key, 7)
    first_key, second_key = jax.random.split(key)
    ndev = NLIST // SLOTS
    drawn = jax.random.randint(first_key, (ndev,), 0, SLOTS)
    skewed = 1 + drawn * drawn // SLOTS
    chosen = jax.random.randint(second_key, (), 0, ndev)
    return jnp.where(jnp.arange(ndev) == chosen, SLOTS, skewed).astype(jnp.int32)


def draw_sites(key, part):
    key = jax.random.fold_in(key, 11)
    first_key, second_key = jax.random.split(key)
    spread = jax.random.randint(first_key, (NLIST,), 0, LX * LY * LZ)
    edge = (LX - 1) * LY * LZ + jax.random.randint(second_key, (NLIST,), 0, LY * LZ)
    leading = jnp.arange(NLIST) % SLOTS == 0
    return jnp.where(leading, edge, spread).astype(jnp.int32)


def block_levels(own_key, extent, shards, smallest, top_value):
    factor_of = 1.0
    for axis_at, blocks in shards:
        heights = jax.random.uniform(jax.random.fold_in(jax.random.fold_in(own_key, 6), axis_at), (blocks,), jnp.float32, smallest / len(shards), top_value / len(shards))
        factor_of = factor_of * jnp.repeat(jnp.exp(heights), extent[axis_at] // blocks).reshape((-1,) + (1,) * (len(extent) - 1 - axis_at))
    return factor_of


def gaussian(key, shape, scale, reach, pieces=(), kind=jnp.bfloat16):
    values = scale * jax.random.normal(key, shape, jnp.float32)
    if pieces:
        values = values * block_levels(key, shape, pieces, -0.22, 0.18)
    return jnp.clip(values, -reach, reach).astype(kind)


def setup_inputs(seed: int = 0, part: int = 0) -> dict:
    key_list = jax.random.split(jax.random.key(seed), 6)
    part_splits = jax.random.split(jax.random.fold_in(key_list[5], part), 6)
    modes = gaussian(part_splits[0], (6, MODES, NSITES), 1.0, 6.0, ((2, 128),))
    links = gaussian(part_splits[1], (3, 18, NSITES), 6 ** -0.5, 2.5, ((2, 128),), jnp.float32)
    sites = draw_sites(jax.random.fold_in(jax.random.fold_in(key_list[5], part), 71), part)
    counts = draw_counts(jax.random.fold_in(jax.random.fold_in(key_list[5], part), 71), part)
    pair_table = jax.random.permutation(key_list[4], NPAIRS).astype(jnp.int32)
    return {"modes": modes, "links": links, "sites": sites, "counts": counts, "pair_table": pair_table}


def build(field, links, at, near, live):
    panels = []
    for k in range(3):
        vec = field[:, :, near[k]].astype(jnp.float32)
        link = links[k][:, at]
        comps = []
        for i in range(3):
            real_part = jnp.zeros(vec.shape[1:], jnp.float32)
            imag_part = jnp.zeros(vec.shape[1:], jnp.float32)
            for j in range(3):
                link_re = link[(i * 3 + j) * 2]
                link_im = link[(i * 3 + j) * 2 + 1]
                real_part = real_part + link_re * vec[2 * j] - link_im * vec[2 * j + 1]
                imag_part = imag_part + link_re * vec[2 * j + 1] + link_im * vec[2 * j]
            comps.append(real_part)
            comps.append(imag_part)
        panels.append(jnp.where(live, jnp.stack(comps), 0.0).astype(jnp.bfloat16))
    return jnp.stack(panels)

def contract(panel, first, second):
    left = panel[0][:, first, :].astype(jnp.float32)
    right = panel[1][:, second, :].astype(jnp.float32)

    def cmul(i, j):
        return (left[2 * i] * right[2 * j] - left[2 * i + 1] * right[2 * j + 1], left[2 * i] * right[2 * j + 1] + left[2 * i + 1] * right[2 * j])
    cross_re = []
    cross_im = []
    for i, j in ((1, 2), (2, 0), (0, 1)):
        plus = cmul(i, j)
        minus = cmul(j, i)
        cross_re.append(plus[0] - minus[0])
        cross_im.append(plus[1] - minus[1])
    w_re = jnp.stack(cross_re).astype(jnp.bfloat16).astype(jnp.float32)
    w_im = jnp.stack(cross_im).astype(jnp.bfloat16).astype(jnp.float32)
    third = panel[2].astype(jnp.float32)
    t_re = third[0::2]
    t_im = third[1::2]

    def inner(u, v):
        return jnp.einsum('cps,cms->pm', u, v)
    return jnp.concatenate([inner(w_re, t_re) - inner(w_im, t_im), inner(w_re, t_im) + inner(w_im, t_re)], axis=1)

def reference(modes, links, sites, counts, pair_table):
    nsites = modes.shape[2]
    plane = LY * LZ
    sdev = LX * plane
    ndev = counts.shape[0]
    slot = jnp.arange(ndev * SLOTS, dtype=jnp.int32)
    owner = slot // SLOTS
    glob = owner * sdev + sites
    ycoord = glob // LZ % LY
    zcoord = glob % LZ
    base = glob - ycoord * LZ - zcoord
    near = [(glob + plane) % nsites, base + (ycoord + 1) % LY * LZ + zcoord, base + ycoord * LZ + (zcoord + 1) % LZ]
    live = slot % SLOTS < counts[owner]
    panel = build(modes, links, glob, near, live)
    blocks = pair_table.reshape(-1, MODES)
    result = lax.map(lambda rows: contract(panel, rows // MODES, rows % MODES), blocks)
    scale = 1.0 / jnp.sqrt(jnp.float32(ndev * SLOTS))
    return result.reshape(-1, 2 * MODES) * scale
```

```python
import jax
import jax.numpy as jnp
from jax import lax
from jax.experimental import pallas as pl
from jax.experimental.pallas import tpu as pltpu
from jax.sharding import PartitionSpec as P

MODES = 96
LY = 16
LZ = 16
PLANE = LY * LZ
SITES = 1024
SLOTS = 24
ROWS = 72
NEAR = 8
FAR = 16
LANES = 128
KWIDE = 256
NEAR_GROUPS = [[NEAR * j + i for i in range(NEAR)] for j in range(FAR)]
FAR_GROUPS = [[NEAR * j + i for j in range(FAR)] for i in range(NEAR)]
PACKED = 112


def build_kernel(sites_ref, counts_ref, modes_ref, ahead_ref, links_ref, out_ref, rows_ref):
    lane = lax.broadcasted_iota(jnp.int32, (1, LANES), 1)
    slot = jnp.where(lane < SLOTS, lane, jnp.where(lane < 2 * SLOTS, lane - SLOTS, lane - 2 * SLOTS))
    site = jnp.zeros((1, LANES), jnp.int32)
    for s in range(SLOTS):
        site = jnp.where(slot == s, sites_ref[s], site)
    z = site & (LZ - 1)
    y = (site >> 4) & (LY - 1)
    base = site - (y << 4) - z
    near = jnp.where(
        lane < SLOTS,
        site + PLANE,
        jnp.where(
            lane < 2 * SLOTS,
            base + (((y + 1) & (LY - 1)) << 4) + z,
            base + (y << 4) + ((z + 1) & (LZ - 1)),
        ),
    )
    used = lane < 3 * SLOTS
    near = jnp.where(used, near, -1)
    at = jnp.where(used, site, -1)
    row = lax.broadcasted_iota(jnp.int32, (SITES, LANES), 0)
    pick = jnp.where(row == near, 1.0, 0.0).astype(jnp.bfloat16)
    pick_ahead = jnp.where(row[:PLANE] + SITES == near, 1.0, 0.0).astype(jnp.bfloat16)
    pick_site = jnp.where(row == at, 1.0, 0.0).astype(jnp.bfloat16)

    field = modes_ref[...].reshape(6 * MODES, SITES)
    ahead = ahead_ref[...].reshape(6 * MODES, PLANE)
    vec = jnp.dot(field, pick, preferred_element_type=jnp.float32) + jnp.dot(
        ahead, pick_ahead, preferred_element_type=jnp.float32
    )

    rows_ref[...] = jnp.zeros_like(rows_ref)
    for k in range(3):
        rows_ref[24 * k : 24 * k + 18, :] = links_ref[k]
    exact = rows_ref[...]
    high = exact.astype(jnp.bfloat16).astype(jnp.float32)
    rest = exact - high
    middle = rest.astype(jnp.bfloat16).astype(jnp.float32)
    low = rest - middle
    split = jnp.concatenate([high, middle, low], axis=0).astype(jnp.bfloat16)
    found = jnp.dot(split, pick_site, preferred_element_type=jnp.float32)
    found = found[0:72] + found[72:144] + found[144:216]
    link = jnp.where(
        lane < SLOTS, found[0:24], jnp.where(lane < 2 * SLOTS, found[24:48], found[48:72])
    )

    live = slot < counts_ref[0]
    turned = []
    for i in range(3):
        real_part = jnp.zeros((MODES, LANES), jnp.float32)
        imag_part = jnp.zeros((MODES, LANES), jnp.float32)
        for j in range(3):
            at_ij = (i * 3 + j) * 2
            link_re = link[at_ij : at_ij + 1]
            link_im = link[at_ij + 1 : at_ij + 2]
            vec_re = vec[2 * j * MODES : (2 * j + 1) * MODES]
            vec_im = vec[(2 * j + 1) * MODES : (2 * j + 2) * MODES]
            real_part = real_part + link_re * vec_re - link_im * vec_im
            imag_part = imag_part + link_re * vec_im + link_im * vec_re
        turned.append(jnp.where(live, real_part, 0.0).T)
        turned.append(jnp.where(live, imag_part, 0.0).T)
    panel = [turned[c][k * SLOTS : (k + 1) * SLOTS] for k in range(3) for c in range(6)]
    out_ref[...] = jnp.concatenate(panel, axis=0).astype(jnp.bfloat16)


def build(sites, counts, modes, ahead, links):
    smem = pl.BlockSpec(memory_space=pltpu.SMEM)
    vmem = pl.BlockSpec(memory_space=pltpu.VMEM)
    return pl.pallas_call(
        build_kernel,
        out_shape=jax.ShapeDtypeStruct((18 * SLOTS, MODES), jnp.bfloat16),
        in_specs=[smem, smem, vmem, vmem, vmem],
        out_specs=vmem,
        scratch_shapes=[pltpu.VMEM((72, SITES), jnp.float32)],
        compiler_params=pltpu.CompilerParams(vmem_limit_bytes=32 << 20),
        name="build_panel",
    )(sites, counts, modes, ahead, links)


def contract_kernel(panel_ref, table_ref, out_ref, side_ref, third_ref, hot_ref, pick_ref, cross_ref):
    total = FAR * ROWS
    lane = lax.broadcasted_iota(jnp.int32, (ROWS, MODES), 1)
    table = table_ref[...].astype(jnp.float32).T.astype(jnp.int32)
    for g in range(FAR):
        pair = table[0:ROWS, g : g + 1]
        first = (pair * 43691) >> 22
        second = pair - first * MODES
        hot_ref[0, g * ROWS : (g + 1) * ROWS, :] = jnp.where(lane == first, 1.0, 0.0)
        hot_ref[1, g * ROWS : (g + 1) * ROWS, :] = jnp.where(lane == second, 1.0, 0.0)

    wide = [panel_ref[d].astype(jnp.float32) for d in range(NEAR)]
    blank = jnp.zeros((KWIDE - NEAR * SLOTS, MODES), jnp.float32)

    def comp(k, c):
        at = (k * 6 + c) * SLOTS
        return jnp.concatenate([w[at : at + SLOTS] for w in wide] + [blank], axis=0)

    for k in range(2):
        for c in range(6):
            side_ref[k * 6 + c] = comp(k, c).astype(jnp.bfloat16)
    for k in range(3):
        t_re = comp(2, 2 * k)
        t_im = comp(2, 2 * k + 1)
        third_ref[2 * k * KWIDE : (2 * k + 1) * KWIDE, :] = jnp.concatenate(
            [t_re, t_im], axis=1
        ).astype(jnp.bfloat16)
        third_ref[(2 * k + 1) * KWIDE : (2 * k + 2) * KWIDE, :] = jnp.concatenate(
            [-t_im, t_re], axis=1
        ).astype(jnp.bfloat16)

    for k in range(2):
        hot = hot_ref[k].astype(jnp.bfloat16)

        @pl.loop(0, 6)
        def _(c):
            pick_ref[k * 6 + c] = lax.dot_general(
                hot, side_ref[k * 6 + c], (((1,), (1,)), ((), ())), preferred_element_type=jnp.float32
            )

    step = 16

    @pl.loop(0, total // step)
    def _(t):
        rows = pl.ds(pl.multiple_of(t * step, step), step)
        left = [pick_ref[c, rows, :] for c in range(6)]
        right = [pick_ref[6 + c, rows, :] for c in range(6)]

        def cmul(i, j):
            return (
                left[2 * i] * right[2 * j] - left[2 * i + 1] * right[2 * j + 1],
                left[2 * i] * right[2 * j + 1] + left[2 * i + 1] * right[2 * j],
            )

        for k, (i, j) in enumerate(((1, 2), (2, 0), (0, 1))):
            plus = cmul(i, j)
            minus = cmul(j, i)
            for r in range(2):
                at = (2 * k + r) * KWIDE
                cross_ref[rows, at : at + KWIDE] = (plus[r] - minus[r]).astype(jnp.bfloat16)

    summed = jnp.dot(cross_ref[...], third_ref[...], preferred_element_type=jnp.float32)
    half = lax.broadcasted_iota(jnp.int32, (40, LANES), 1) < 64
    for g in range(FAR):
        mine = summed[g * ROWS : (g + 1) * ROWS]
        tail = jnp.concatenate(
            [mine[:, LANES:], jnp.zeros((ROWS, 64), jnp.float32)], axis=1
        )
        lower = jnp.concatenate([tail[40:72], jnp.zeros((8, LANES), jnp.float32)], axis=0)
        packed = jnp.where(half, tail[0:40], pltpu.roll(lower, 64, 1))
        out_ref[g] = jnp.concatenate([mine[:, :LANES], packed], axis=0).astype(jnp.bfloat16)


def contract(panels, table):
    vmem = pl.BlockSpec(memory_space=pltpu.VMEM)
    total = FAR * ROWS
    return pl.pallas_call(
        contract_kernel,
        out_shape=jax.ShapeDtypeStruct((FAR, PACKED, LANES), jnp.bfloat16),
        in_specs=[vmem, vmem],
        out_specs=vmem,
        scratch_shapes=[
            pltpu.VMEM((12, KWIDE, MODES), jnp.bfloat16),
            pltpu.VMEM((6 * KWIDE, 2 * MODES), jnp.bfloat16),
            pltpu.VMEM((2, total, MODES), jnp.float32),
            pltpu.VMEM((12, total, KWIDE), jnp.float32),
            pltpu.VMEM((total, 6 * KWIDE), jnp.bfloat16),
        ],
        compiler_params=pltpu.CompilerParams(vmem_limit_bytes=48 << 20),
        name="contract_pairs",
    )(panels, table)


def total_kernel(scale, parts_ref, out_ref):
    total = parts_ref[0].astype(jnp.float32)
    for g in range(1, FAR):
        total = total + parts_ref[g].astype(jnp.float32)
    total = total * scale
    out_ref[:, 0:LANES] = total[0:ROWS]
    out_ref[0:40, LANES : 2 * MODES] = total[ROWS : ROWS + 40, 0:64]
    out_ref[40:72, LANES : 2 * MODES] = pltpu.roll(total[ROWS : ROWS + 32], 64, 1)[:, 0:64]


def add_up(parts):
    vmem = pl.BlockSpec(memory_space=pltpu.VMEM)
    scale = float(1.0 / (NEAR * FAR * SLOTS) ** 0.5)
    return pl.pallas_call(
        lambda *refs: total_kernel(scale, *refs),
        out_shape=jax.ShapeDtypeStruct((ROWS, 2 * MODES), jnp.float32),
        in_specs=[vmem],
        out_specs=vmem,
        name="add_up",
    )(parts)


def shards(modes, links, sites, counts, pair_table):
    count = lax.axis_size("gx")
    pairs = [(source, (source - 1) % count) for source in range(count)]
    ahead = lax.ppermute(modes[:, :, :PLANE], "gx", pairs)
    padded = jnp.pad(pair_table, (0, LANES - ROWS))
    tables = lax.all_to_all(
        jnp.broadcast_to(padded, (FAR, LANES)), "gx", 0, 0, axis_index_groups=FAR_GROUPS
    )
    panel = build(sites, counts, modes, ahead, links)
    panels = lax.all_gather(panel, "gx", axis_index_groups=NEAR_GROUPS)
    parts = contract(panels, tables)
    parts = lax.all_to_all(parts, "gx", 0, 0, axis_index_groups=FAR_GROUPS)
    return add_up(parts)


def solution(mesh):
    placed = (P("ta", None, "gx"), P("ta", None, "gx"), P(("ta", "gx")), P(("ta", "gx")), P("gx"))
    return jax.shard_map(
        shards, mesh=mesh, in_specs=placed, out_specs=P(("ta", "gx"), None), check_vma=False
    )
```

```python
import jax
import jax.numpy as jnp
from jax import lax
from jax.experimental import pallas as pl
from jax.experimental.pallas import tpu as pltpu
from jax.sharding import PartitionSpec as P

MODES = 96
LY = 16
LZ = 16
PLANE = LY * LZ
SITES = 1024
SLOTS = 24
ROWS = 72
NEAR = 8
FAR = 16
LANES = 128
KWIDE = 256
FAR_GROUPS = [[NEAR * j + i for j in range(FAR)] for i in range(NEAR)]
PACKED = 112
WIRE = 336


def local_kernel(
    sites_hbm, counts_ref, modes_hbm, links_hbm, vec_ref, link_ref, marks_ref,
    sites_ref, modes_ref, links_ref, rows_ref, sems,
):
    copies = [
        pltpu.make_async_copy(sites_hbm, sites_ref, sems.at[0]),
        pltpu.make_async_copy(links_hbm, links_ref, sems.at[1]),
    ] + [pltpu.make_async_copy(modes_hbm.at[c], modes_ref.at[c], sems.at[2 + c]) for c in range(6)]
    for copy in copies:
        copy.start()
    lane = lax.broadcasted_iota(jnp.int32, (1, LANES), 1)
    slot = jnp.where(lane < SLOTS, lane, jnp.where(lane < 2 * SLOTS, lane - SLOTS, lane - 2 * SLOTS))
    copies[0].wait()
    site = jnp.zeros((1, LANES), jnp.int32)
    for s in range(SLOTS):
        site = jnp.where(slot == s, sites_ref[s], site)
    z = site & (LZ - 1)
    y = (site >> 4) & (LY - 1)
    base = site - (y << 4) - z
    near = jnp.where(
        lane < SLOTS,
        site + PLANE,
        jnp.where(
            lane < 2 * SLOTS,
            base + (((y + 1) & (LY - 1)) << 4) + z,
            base + (y << 4) + ((z + 1) & (LZ - 1)),
        ),
    )
    used = lane < 3 * SLOTS
    near = jnp.where(used, near, -1)
    at = jnp.where(used, site, -1)
    marks_ref[0:1, :] = near - SITES
    marks_ref[1:2, :] = jnp.where(slot < counts_ref[0], 1, 0)
    row = lax.broadcasted_iota(jnp.int32, (SITES, LANES), 0)
    pick = jnp.where(row == near, 1.0, 0.0).astype(jnp.bfloat16)
    pick_site = jnp.where(row == at, 1.0, 0.0).astype(jnp.bfloat16)

    rows_ref[...] = jnp.zeros_like(rows_ref)
    copies[1].wait()
    for k in range(3):
        rows_ref[24 * k : 24 * k + 18, :] = links_ref[k]
    exact = rows_ref[...]
    high = exact.astype(jnp.bfloat16).astype(jnp.float32)
    rest = exact - high
    middle = rest.astype(jnp.bfloat16).astype(jnp.float32)
    low = rest - middle
    split = jnp.concatenate([high, middle, low], axis=0).astype(jnp.bfloat16)
    found = jnp.dot(split, pick_site, preferred_element_type=jnp.float32)
    found = found[0:72] + found[72:144] + found[144:216]
    link_ref[...] = jnp.where(
        lane < SLOTS, found[0:24], jnp.where(lane < 2 * SLOTS, found[24:48], found[48:72])
    )
    for c in range(6):
        copies[2 + c].wait()
    field = modes_ref[...].reshape(6 * MODES, SITES)
    vec_ref[...] = jnp.dot(field, pick, preferred_element_type=jnp.float32)


def pinned(value):
    return pltpu.with_memory_space_constraint(value, pltpu.HBM)


def build_local(sites, counts, modes, links):
    vmem = pl.BlockSpec(memory_space=pltpu.VMEM)
    hbm = pl.BlockSpec(memory_space=pltpu.HBM)
    return pl.pallas_call(
        local_kernel,
        out_shape=(
            pltpu.VMEM((6 * MODES, LANES), jnp.float32),
            pltpu.VMEM((24, LANES), jnp.float32),
            pltpu.VMEM((8, LANES), jnp.int32),
        ),
        in_specs=[hbm, pl.BlockSpec(memory_space=pltpu.SMEM), hbm, hbm],
        out_specs=(vmem, vmem, vmem),
        scratch_shapes=[
            pltpu.SMEM((SLOTS,), jnp.int32),
            pltpu.VMEM((6, MODES, SITES), jnp.bfloat16),
            pltpu.VMEM((3, 18, SITES), jnp.float32),
            pltpu.VMEM((72, SITES), jnp.float32),
            pltpu.SemaphoreType.DMA((8,)),
        ],
        compiler_params=pltpu.CompilerParams(vmem_limit_bytes=16 << 20),
        cost_estimate=pl.CostEstimate(flops=200_000_000, bytes_accessed=6_000_000, transcendentals=0),
        name="local_vectors",
    )(pinned(sites), counts, pinned(modes), pinned(links))


def build_kernel(vec_ref, link_ref, marks_ref, ahead_ref, out_ref):
    row = lax.broadcasted_iota(jnp.int32, (PLANE, LANES), 0)
    pick_ahead = jnp.where(row == marks_ref[0:1, :], 1.0, 0.0).astype(jnp.bfloat16)
    ahead = ahead_ref[...].reshape(6 * MODES, PLANE)
    vec = vec_ref[...] + jnp.dot(ahead, pick_ahead, preferred_element_type=jnp.float32)
    live = marks_ref[1:2, :] > 0
    link = link_ref[...]
    blank = jnp.zeros((LANES - MODES, LANES), jnp.float32)
    turned = []
    for i in range(3):
        real_part = jnp.zeros((MODES, LANES), jnp.float32)
        imag_part = jnp.zeros((MODES, LANES), jnp.float32)
        for j in range(3):
            at_ij = (i * 3 + j) * 2
            link_re = link[at_ij : at_ij + 1]
            link_im = link[at_ij + 1 : at_ij + 2]
            vec_re = vec[2 * j * MODES : (2 * j + 1) * MODES]
            vec_im = vec[(2 * j + 1) * MODES : (2 * j + 2) * MODES]
            real_part = real_part + link_re * vec_re - link_im * vec_im
            imag_part = imag_part + link_re * vec_im + link_im * vec_re
        for part in (real_part, imag_part):
            turned.append(jnp.concatenate([jnp.where(live, part, 0.0), blank], axis=0).T)
    panel = [turned[c][k * SLOTS : (k + 1) * SLOTS] for k in range(3) for c in range(6)]
    main = jnp.concatenate(panel[:14], axis=0)
    tail = jnp.concatenate(panel[14:], axis=0)
    spread = jnp.concatenate(
        [pltpu.roll(tail, 96, 1), pltpu.roll(tail, 64, 1), pltpu.roll(tail, 32, 1),
         jnp.zeros((WIRE - 288, LANES), jnp.float32)],
        axis=0,
    )
    lane = lax.broadcasted_iota(jnp.int32, (1, LANES), 1)
    out_ref[...] = jnp.where(lane < MODES, main, spread).astype(jnp.bfloat16)


def build(vec, link, marks, ahead):
    vmem = pl.BlockSpec(memory_space=pltpu.VMEM)
    return pl.pallas_call(
        build_kernel,
        out_shape=jax.ShapeDtypeStruct((WIRE, LANES), jnp.bfloat16),
        in_specs=[vmem] * 4,
        out_specs=vmem,
        compiler_params=pltpu.CompilerParams(vmem_limit_bytes=16 << 20),
        name="build_panel",
    )(vec, link, marks, ahead)


def contract_kernel(*refs):
    panel_refs, (table_ref, out_ref, side_ref, third_ref, pick_ref, cross_ref) = refs[:NEAR], refs[NEAR:]
    total = FAR * ROWS
    lane = lax.broadcasted_iota(jnp.int32, (1, LANES), 1)
    table = jnp.concatenate(
        [table_ref[...].astype(jnp.float32), jnp.zeros((FAR, LANES - ROWS), jnp.float32)], axis=1
    ).T.astype(jnp.int32)
    first_hot = []
    second_hot = []
    for g in range(FAR):
        pair = table[0:ROWS, g : g + 1]
        first = (pair * 43691) >> 22
        second = pair - first * MODES
        first_hot.append(jnp.where(lane == first, 1.0, 0.0))
        second_hot.append(jnp.where(lane == second, 1.0, 0.0))
    hots = [jnp.concatenate(h, axis=0).astype(jnp.bfloat16) for h in (first_hot, second_hot)]

    blank = jnp.zeros((KWIDE - NEAR * SLOTS, LANES), jnp.float32)
    comps = [[] for _ in range(18)]
    for ref in panel_refs:
        wide = ref[...].astype(jnp.float32)
        for n in range(14):
            comps[n].append(wide[n * SLOTS : (n + 1) * SLOTS])
        tail = jnp.where(
            lane < 32,
            pltpu.roll(wide[0:96], 32, 1),
            jnp.where(lane < 64, pltpu.roll(wide[96:192], 64, 1), pltpu.roll(wide[192:288], 96, 1)),
        )
        for n in range(4):
            comps[14 + n].append(tail[n * SLOTS : (n + 1) * SLOTS])
    for n in range(12):
        side_ref[n] = jnp.concatenate(comps[n] + [blank], axis=0).astype(jnp.bfloat16)
    for k in range(3):
        t_re = jnp.concatenate(comps[12 + 2 * k] + [blank], axis=0)
        t_im = jnp.concatenate(comps[13 + 2 * k] + [blank], axis=0)
        for r, (left, right) in enumerate(((t_re, t_im), (-t_im, t_re))):
            at = (2 * k + r) * KWIDE
            moved = pltpu.roll(right, 96, 1)
            third_ref[at : at + KWIDE, 0:LANES] = jnp.where(lane < 96, left, moved).astype(jnp.bfloat16)
            third_ref[at : at + KWIDE, LANES : 2 * LANES] = moved.astype(jnp.bfloat16)

    for k in range(2):
        hot = hots[k]

        @pl.loop(0, 6)
        def _(c):
            pick_ref[k * 6 + c] = lax.dot_general(
                hot, side_ref[k * 6 + c], (((1,), (1,)), ((), ())), preferred_element_type=jnp.float32
            )

    step = 16

    @pl.loop(0, total // step)
    def _(t):
        rows = pl.ds(pl.multiple_of(t * step, step), step)
        left = [pick_ref[c, rows, :] for c in range(6)]
        right = [pick_ref[6 + c, rows, :] for c in range(6)]

        def cmul(i, j):
            return (
                left[2 * i] * right[2 * j] - left[2 * i + 1] * right[2 * j + 1],
                left[2 * i] * right[2 * j + 1] + left[2 * i + 1] * right[2 * j],
            )

        for k, (i, j) in enumerate(((1, 2), (2, 0), (0, 1))):
            plus = cmul(i, j)
            minus = cmul(j, i)
            for r in range(2):
                at = (2 * k + r) * KWIDE
                cross_ref[rows, at : at + KWIDE] = (plus[r] - minus[r]).astype(jnp.bfloat16)

    half = lax.broadcasted_iota(jnp.int32, (40, LANES), 1) < 64
    summed = jnp.dot(cross_ref[...], third_ref[...], preferred_element_type=jnp.float32)
    for g in range(FAR):
        mine = summed[g * ROWS : (g + 1) * ROWS]
        tail = mine[:, LANES:]
        lower = jnp.concatenate([tail[40:72], jnp.zeros((8, LANES), jnp.float32)], axis=0)
        packed = jnp.where(half, tail[0:40], pltpu.roll(lower, 64, 1))
        out_ref[g] = jnp.concatenate([mine[:, :LANES], packed], axis=0).astype(jnp.bfloat16)


def contract(panels, table):
    vmem = pl.BlockSpec(memory_space=pltpu.VMEM)
    total = FAR * ROWS
    return pl.pallas_call(
        contract_kernel,
        out_shape=jax.ShapeDtypeStruct((FAR, PACKED, LANES), jnp.bfloat16),
        in_specs=[vmem] * (NEAR + 1),
        out_specs=vmem,
        scratch_shapes=[
            pltpu.VMEM((12, KWIDE, LANES), jnp.bfloat16),
            pltpu.VMEM((6 * KWIDE, 2 * LANES), jnp.bfloat16),
            pltpu.VMEM((12, total, KWIDE), jnp.float32),
            pltpu.VMEM((total, 6 * KWIDE), jnp.bfloat16),
        ],
        compiler_params=pltpu.CompilerParams(vmem_limit_bytes=48 << 20),
        name="contract_pairs",
    )(*panels, table)


def total_kernel(scale, parts_ref, out_ref):
    total = parts_ref[0].astype(jnp.float32)
    for g in range(1, FAR):
        total = total + parts_ref[g].astype(jnp.float32)
    total = total * scale
    out_ref[:, 0:LANES] = total[0:ROWS]
    out_ref[0:40, LANES : 2 * MODES] = total[ROWS : ROWS + 40, 0:64]
    out_ref[40:72, LANES : 2 * MODES] = pltpu.roll(total[ROWS : ROWS + 32], 64, 1)[:, 0:64]


def add_up(parts):
    vmem = pl.BlockSpec(memory_space=pltpu.VMEM)
    scale = float(1.0 / (NEAR * FAR * SLOTS) ** 0.5)
    return pl.pallas_call(
        lambda *refs: total_kernel(scale, *refs),
        out_shape=jax.ShapeDtypeStruct((ROWS, 2 * MODES), jnp.float32),
        in_specs=[vmem],
        out_specs=vmem,
        compiler_params=pltpu.CompilerParams(vmem_limit_bytes=8 << 20),
        name="add_up",
    )(parts)


def swapped(value, bits):
    count = lax.axis_size("gx")
    return lax.ppermute(value, "gx", [(source, source ^ bits) for source in range(count)])


def shards(modes, links, sites, counts, pair_table):
    count = lax.axis_size("gx")
    pairs = [(source, (source - 1) % count) for source in range(count)]
    ahead = lax.ppermute(modes[:, :, :PLANE], "gx", pairs)
    tables = lax.all_to_all(
        jnp.broadcast_to(pair_table, (FAR, ROWS)), "gx", 0, 0, axis_index_groups=FAR_GROUPS
    )
    vec, link, marks = build_local(sites, counts, modes, links)
    panel = build(vec, link, marks, ahead)
    panel, tables = lax.optimization_barrier((panel, tables))
    others = [swapped(panel, bits) for bits in (2, 4, 6)]
    panels = [panel] + others
    panels = panels + [swapped(p, 1) for p in panels]
    parts = contract(panels, tables)
    parts = lax.all_to_all(parts, "gx", 0, 0, axis_index_groups=FAR_GROUPS)
    return add_up(parts)


def solution(mesh):
    placed = (P("ta", None, "gx"), P("ta", None, "gx"), P(("ta", "gx")), P(("ta", "gx")), P("gx"))
    return jax.shard_map(
        shards, mesh=mesh, in_specs=placed, out_specs=P(("ta", "gx"), None), check_vma=False
    )
```

```python
import jax
import jax.numpy as jnp
from jax import lax
from jax.experimental import pallas as pl
from jax.experimental.pallas import tpu as pltpu
from jax.sharding import PartitionSpec as P

MODES = 96
LY = 16
LZ = 16
PLANE = LY * LZ
SITES = 1024
SLOTS = 24
ROWS = 72
NEAR = 8
FAR = 16
LANES = 128
FAR_GROUPS = [[NEAR * j + i for j in range(FAR)] for i in range(NEAR)]
PACKED = 112
WIRE = 336


def pinned(value):
    return pltpu.with_memory_space_constraint(value, pltpu.HBM)


def prepare_kernel(table_hbm, modes_hbm, plane_ref, tables_ref, table_ref, sems):
    small = pltpu.make_async_copy(table_hbm, table_ref, sems.at[0])
    small.start()
    copy = pltpu.make_async_copy(modes_hbm.at[:, :, pl.ds(0, PLANE)], plane_ref, sems.at[1])
    copy.start()
    small.wait()
    row = jnp.concatenate([table_ref[...], jnp.zeros((1, LANES - ROWS), jnp.int32)], axis=1)
    for g in range(FAR):
        tables_ref[g] = jnp.broadcast_to(row, (16, LANES))
    copy.wait()


def prepare(modes, pair_table):
    vmem = pl.BlockSpec(memory_space=pltpu.VMEM)
    return pl.pallas_call(
        prepare_kernel,
        out_shape=(
            pltpu.VMEM((6, MODES, PLANE), jnp.bfloat16),
            pltpu.VMEM((FAR, 16, LANES), jnp.int32),
        ),
        in_specs=[pl.BlockSpec(memory_space=pltpu.HBM)] * 2,
        out_specs=(vmem, vmem),
        scratch_shapes=[pltpu.VMEM((1, ROWS), jnp.int32), pltpu.SemaphoreType.DMA((2,))],
        compiler_params=pltpu.CompilerParams(vmem_limit_bytes=8 << 20),
        name="prepare",
    )(pinned(pair_table.reshape(1, ROWS)), pinned(modes))


def local_kernel(
    sites_hbm, counts_ref, modes_hbm, links_hbm, vec_ref, link_ref, marks_ref,
    sites_ref, modes_ref, links_ref, rows_ref, sems,
):
    copies = [
        pltpu.make_async_copy(sites_hbm, sites_ref, sems.at[0]),
        pltpu.make_async_copy(links_hbm, links_ref, sems.at[1]),
    ] + [pltpu.make_async_copy(modes_hbm.at[c], modes_ref.at[c], sems.at[2 + c]) for c in range(6)]
    for copy in copies:
        copy.start()
    lane = lax.broadcasted_iota(jnp.int32, (1, LANES), 1)
    slot = jnp.where(lane < SLOTS, lane, jnp.where(lane < 2 * SLOTS, lane - SLOTS, lane - 2 * SLOTS))
    copies[0].wait()
    site = jnp.zeros((1, LANES), jnp.int32)
    for s in range(SLOTS):
        site = jnp.where(slot == s, sites_ref[s], site)
    z = site & (LZ - 1)
    y = (site >> 4) & (LY - 1)
    base = site - (y << 4) - z
    near = jnp.where(
        lane < SLOTS,
        site + PLANE,
        jnp.where(
            lane < 2 * SLOTS,
            base + (((y + 1) & (LY - 1)) << 4) + z,
            base + (y << 4) + ((z + 1) & (LZ - 1)),
        ),
    )
    used = lane < 3 * SLOTS
    near = jnp.where(used, near, -1)
    at = jnp.where(used, site, -1)
    marks_ref[0:1, :] = near - SITES
    marks_ref[1:2, :] = jnp.where(slot < counts_ref[0], 1, 0)
    row = lax.broadcasted_iota(jnp.int32, (SITES, LANES), 0)
    pick = jnp.where(row == near, 1.0, 0.0).astype(jnp.bfloat16)
    pick_site = jnp.where(row == at, 1.0, 0.0).astype(jnp.bfloat16)

    rows_ref[...] = jnp.zeros_like(rows_ref)
    copies[1].wait()
    for k in range(3):
        rows_ref[24 * k : 24 * k + 18, :] = links_ref[k]
    exact = rows_ref[...]
    high = exact.astype(jnp.bfloat16).astype(jnp.float32)
    rest = exact - high
    middle = rest.astype(jnp.bfloat16).astype(jnp.float32)
    low = rest - middle
    split = jnp.concatenate([high, middle, low], axis=0).astype(jnp.bfloat16)
    found = jnp.dot(split, pick_site, preferred_element_type=jnp.float32)
    found = found[0:72] + found[72:144] + found[144:216]
    link_ref[...] = jnp.where(
        lane < SLOTS, found[0:24], jnp.where(lane < 2 * SLOTS, found[24:48], found[48:72])
    )
    for c in range(6):
        copies[2 + c].wait()
    field = modes_ref[...].reshape(6 * MODES, SITES)
    vec_ref[...] = jnp.dot(field, pick, preferred_element_type=jnp.float32)


def build_local(sites, counts, modes, links):
    vmem = pl.BlockSpec(memory_space=pltpu.VMEM)
    hbm = pl.BlockSpec(memory_space=pltpu.HBM)
    return pl.pallas_call(
        local_kernel,
        out_shape=(
            pltpu.VMEM((6 * MODES, LANES), jnp.float32),
            pltpu.VMEM((24, LANES), jnp.float32),
            pltpu.VMEM((8, LANES), jnp.int32),
        ),
        in_specs=[hbm, pl.BlockSpec(memory_space=pltpu.SMEM), hbm, hbm],
        out_specs=(vmem, vmem, vmem),
        scratch_shapes=[
            pltpu.SMEM((SLOTS,), jnp.int32),
            pltpu.VMEM((6, MODES, SITES), jnp.bfloat16),
            pltpu.VMEM((3, 18, SITES), jnp.float32),
            pltpu.VMEM((72, SITES), jnp.float32),
            pltpu.SemaphoreType.DMA((8,)),
        ],
        compiler_params=pltpu.CompilerParams(vmem_limit_bytes=16 << 20),
        cost_estimate=pl.CostEstimate(flops=200_000_000, bytes_accessed=6_000_000, transcendentals=0),
        name="local_vectors",
    )(pinned(sites), counts, pinned(modes), pinned(links))


def build_kernel(vec_ref, link_ref, marks_ref, ahead_ref, out_ref):
    row = lax.broadcasted_iota(jnp.int32, (PLANE, LANES), 0)
    pick_ahead = jnp.where(row == marks_ref[0:1, :], 1.0, 0.0).astype(jnp.bfloat16)
    ahead = ahead_ref[...].reshape(6 * MODES, PLANE)
    vec = vec_ref[...] + jnp.dot(ahead, pick_ahead, preferred_element_type=jnp.float32)
    live = marks_ref[1:2, :] > 0
    link = link_ref[...]
    blank = jnp.zeros((LANES - MODES, LANES), jnp.float32)
    turned = []
    for i in range(3):
        real_part = jnp.zeros((MODES, LANES), jnp.float32)
        imag_part = jnp.zeros((MODES, LANES), jnp.float32)
        for j in range(3):
            at_ij = (i * 3 + j) * 2
            link_re = link[at_ij : at_ij + 1]
            link_im = link[at_ij + 1 : at_ij + 2]
            vec_re = vec[2 * j * MODES : (2 * j + 1) * MODES]
            vec_im = vec[(2 * j + 1) * MODES : (2 * j + 2) * MODES]
            real_part = real_part + link_re * vec_re - link_im * vec_im
            imag_part = imag_part + link_re * vec_im + link_im * vec_re
        for part in (real_part, imag_part):
            turned.append(jnp.concatenate([jnp.where(live, part, 0.0), blank], axis=0).T)
    panel = [turned[c][k * SLOTS : (k + 1) * SLOTS] for k in range(3) for c in range(6)]
    main = jnp.concatenate(panel[:14], axis=0)
    tail = jnp.concatenate(panel[14:], axis=0)
    spread = jnp.concatenate(
        [pltpu.roll(tail, 96, 1), pltpu.roll(tail, 64, 1), pltpu.roll(tail, 32, 1),
         jnp.zeros((WIRE - 288, LANES), jnp.float32)],
        axis=0,
    )
    lane = lax.broadcasted_iota(jnp.int32, (1, LANES), 1)
    out_ref[...] = jnp.where(lane < MODES, main, spread).astype(jnp.bfloat16)


def build(vec, link, marks, ahead):
    vmem = pl.BlockSpec(memory_space=pltpu.VMEM)
    return pl.pallas_call(
        build_kernel,
        out_shape=jax.ShapeDtypeStruct((WIRE, LANES), jnp.bfloat16),
        in_specs=[vmem] * 4,
        out_specs=vmem,
        compiler_params=pltpu.CompilerParams(vmem_limit_bytes=16 << 20),
        name="build_panel",
    )(vec, link, marks, ahead)


TILES = ((0, 256), (256, 256), (512, 256), (768, 256), (1024, 128))
SHARED = NEAR * SLOTS
STACK = 6 * SHARED


def contract_kernel(*refs):
    panel_refs = refs[:NEAR]
    table_ref, out_ref, side_ref, third_ref, *scratch = refs[NEAR:]
    pick_refs, cross_refs = scratch[:4], scratch[4:]
    lane = lax.broadcasted_iota(jnp.int32, (1, LANES), 1)

    rows = [table_ref[g][0:1] for g in range(FAR)]
    pieces = [
        jnp.where(lane < 64, rows[2 * v], pltpu.roll(rows[2 * v + 1], 64, 1)) for v in range(FAR // 2)
    ]
    last = jnp.zeros((1, LANES), jnp.int32)
    for g in range(FAR):
        moved = pltpu.roll(rows[g], (8 * g - 64) % LANES, 1) if g != 8 else rows[g]
        last = jnp.where((lane >= 8 * g) & (lane < 8 * g + 8), moved, last)
    pairs = jnp.concatenate(pieces + [last], axis=1)
    first = (pairs * 43691) >> 22
    second = pairs - first * MODES

    comps = [[] for _ in range(18)]
    for ref in panel_refs:
        wide = ref[...].astype(jnp.float32)
        for n in range(14):
            comps[n].append(wide[n * SLOTS : (n + 1) * SLOTS])
        tail = jnp.where(
            lane < 32,
            pltpu.roll(wide[0:96], 32, 1),
            jnp.where(lane < 64, pltpu.roll(wide[96:192], 64, 1), pltpu.roll(wide[192:288], 96, 1)),
        )
        for n in range(4):
            comps[14 + n].append(tail[n * SLOTS : (n + 1) * SLOTS])
    comps = [jnp.concatenate(c, axis=0) for c in comps]
    for n in range(12):
        side_ref[n // 6, (n % 6) * SHARED : (n % 6 + 1) * SHARED, :] = comps[n].astype(jnp.bfloat16)

    def third():
        upper = []
        lower = []
        for k in range(3):
            t_re, t_im = comps[12 + 2 * k], comps[13 + 2 * k]
            upper += [t_re, -t_im]
            lower += [t_im, t_re]
        third_ref[0:MODES, :] = jnp.concatenate(upper, axis=0).T[0:MODES].astype(jnp.bfloat16)
        third_ref[MODES : 2 * MODES, :] = jnp.concatenate(lower, axis=0).T[0:MODES].astype(jnp.bfloat16)

    half = lane < 64

    def select(t):
        at, width = TILES[t]
        mode = lax.broadcasted_iota(jnp.int32, (LANES, width), 0)
        for n, index in enumerate((first, second)):
            hot = jnp.where(mode == index[:, at : at + width], 1.0, 0.0).astype(jnp.bfloat16)
            pick_refs[2 * (t % 2) + n][:, 0:width] = jnp.dot(
                side_ref[n], hot, preferred_element_type=jnp.float32
            )

    def cross(t):
        at, width = TILES[t]
        lefts, rights, target = pick_refs[2 * (t % 2)], pick_refs[2 * (t % 2) + 1], cross_refs[t % 2]

        def chunk(q):
            left = [lefts[pl.ds(c * SHARED + q, 16), 0:width] for c in range(6)]
            right = [rights[pl.ds(c * SHARED + q, 16), 0:width] for c in range(6)]

            def cmul(i, j):
                return (
                    left[2 * i] * right[2 * j] - left[2 * i + 1] * right[2 * j + 1],
                    left[2 * i] * right[2 * j + 1] + left[2 * i + 1] * right[2 * j],
                )

            for k, (i, j) in enumerate(((1, 2), (2, 0), (0, 1))):
                plus = cmul(i, j)
                minus = cmul(j, i)
                for r in range(2):
                    target[pl.ds((2 * k + r) * SHARED + q, 16), 0:width] = (plus[r] - minus[r]).astype(
                        jnp.bfloat16
                    )

        for q in range(0, SHARED, 16):
            chunk(q)

    def finish(t):
        at, width = TILES[t]
        summed = jnp.dot(
            third_ref[...], cross_refs[t % 2][:, 0:width], preferred_element_type=jnp.float32
        )
        if width == LANES:
            flat = jnp.concatenate([summed, jnp.zeros((64, LANES), jnp.float32)], axis=0)
            low, high = flat[0:LANES].T, flat[LANES : 2 * LANES].T
            for g in range(FAR):
                both = [low[8 * g : 8 * g + 8], high[8 * g : 8 * g + 8]]
                out_ref[g, MODES : MODES + 16, :] = jnp.concatenate(both, axis=0).astype(jnp.bfloat16)
            return
        for v in range(2):
            real = summed[0:MODES, v * LANES : (v + 1) * LANES]
            imag = summed[MODES : 2 * MODES, v * LANES : (v + 1) * LANES]
            g = at // 64 + 2 * v
            out_ref[g, 0:MODES, :] = jnp.where(half, real, pltpu.roll(imag, 64, 1)).astype(jnp.bfloat16)
            out_ref[g + 1, 0:MODES, :] = jnp.where(half, pltpu.roll(real, 64, 1), imag).astype(
                jnp.bfloat16
            )

    select(0)
    third()
    for t in range(len(TILES)):
        if t + 1 < len(TILES):
            select(t + 1)
        cross(t)
        finish(t)


def contract(panels, tables):
    vmem = pl.BlockSpec(memory_space=pltpu.VMEM)
    return pl.pallas_call(
        contract_kernel,
        out_shape=jax.ShapeDtypeStruct((FAR, PACKED, LANES), jnp.bfloat16),
        in_specs=[vmem] * (NEAR + 1),
        out_specs=vmem,
        scratch_shapes=[
            pltpu.VMEM((2, STACK, LANES), jnp.bfloat16),
            pltpu.VMEM((2 * MODES, STACK), jnp.bfloat16),
        ]
        + [pltpu.VMEM((STACK, 256), jnp.float32)] * 4
        + [pltpu.VMEM((STACK, 256), jnp.bfloat16)] * 2,
        compiler_params=pltpu.CompilerParams(vmem_limit_bytes=40 << 20),
        name="contract_pairs",
    )(*panels, tables)


def total_kernel(scale, parts_ref, out_ref):
    total = parts_ref[0].astype(jnp.float32)
    for g in range(1, FAR):
        total = total + parts_ref[g].astype(jnp.float32)
    total = total * scale
    lane = lax.broadcasted_iota(jnp.int32, (1, LANES), 1)
    main = jnp.concatenate([total[0:MODES], jnp.zeros((LANES - MODES, LANES), jnp.float32)], axis=0).T
    moved = pltpu.roll(main[64:128], 96, 1)
    out_ref[0:64, 0:LANES] = jnp.where(lane < MODES, main[0:64], moved)
    out_ref[0:64, LANES : 2 * MODES] = moved[:, 0:64]
    out_ref[64:72, 0:LANES] = total[MODES : MODES + 8]
    out_ref[64:72, LANES : 2 * MODES] = total[MODES + 8 : MODES + 16, 0:64]


def add_up(parts):
    vmem = pl.BlockSpec(memory_space=pltpu.VMEM)
    scale = float(1.0 / (NEAR * FAR * SLOTS) ** 0.5)
    return pl.pallas_call(
        lambda *refs: total_kernel(scale, *refs),
        out_shape=jax.ShapeDtypeStruct((ROWS, 2 * MODES), jnp.float32),
        in_specs=[vmem],
        out_specs=vmem,
        compiler_params=pltpu.CompilerParams(vmem_limit_bytes=8 << 20),
        name="add_up",
    )(parts)


def swapped(value, bits):
    count = lax.axis_size("gx")
    return lax.ppermute(value, "gx", [(source, source ^ bits) for source in range(count)])


def shards(modes, links, sites, counts, pair_table):
    count = lax.axis_size("gx")
    pairs = [(source, (source - 1) % count) for source in range(count)]
    plane, tables = prepare(modes, pair_table)
    ahead = lax.ppermute(plane, "gx", pairs)
    tables = lax.all_to_all(tables, "gx", 0, 0, axis_index_groups=FAR_GROUPS)
    vec, link, marks = build_local(sites, counts, modes, links)
    panel = build(vec, link, marks, ahead)
    others = [swapped(panel, bits) for bits in (2, 4, 6)]
    panels = [panel] + others
    panels = panels + [swapped(p, 1) for p in panels]
    parts = contract(panels, tables)
    parts = lax.all_to_all(parts, "gx", 0, 0, axis_index_groups=FAR_GROUPS)
    return add_up(parts)


def solution(mesh):
    placed = (P("ta", None, "gx"), P("ta", None, "gx"), P(("ta", "gx")), P(("ta", "gx")), P("gx"))
    return jax.shard_map(
        shards, mesh=mesh, in_specs=placed, out_specs=P(("ta", "gx"), None), check_vma=False
    )
```

```python
import jax
import jax.numpy as jnp
from jax import lax
from jax.experimental import pallas as pl
from jax.experimental.pallas import tpu as pltpu
from jax.sharding import PartitionSpec as P

MODES = 96
LY = 16
LZ = 16
PLANE = LY * LZ
SITES = 1024
SLOTS = 24
ROWS = 72
NEAR = 8
FAR = 16
LANES = 128
FAR_GROUPS = [[NEAR * j + i for j in range(FAR)] for i in range(NEAR)]
PACKED = 112
WIRE = 336


def pinned(value):
    return pltpu.with_memory_space_constraint(value, pltpu.HBM)


def local_kernel(
    table_hbm, sites_hbm, modes_hbm, links_hbm, plane_ref, tables_ref, vec_ref, link_ref, marks_ref,
    table_ref, sites_ref, modes_ref, links_ref, rows_ref, sems,
):
    copies = [
        pltpu.make_async_copy(sites_hbm, sites_ref, sems.at[0]),
        pltpu.make_async_copy(links_hbm, links_ref, sems.at[1]),
    ] + [pltpu.make_async_copy(modes_hbm.at[c], modes_ref.at[c], sems.at[2 + c]) for c in range(6)]
    table_copy = pltpu.make_async_copy(table_hbm, table_ref, sems.at[8])
    table_copy.start()
    for copy in copies:
        copy.start()
    lane = lax.broadcasted_iota(jnp.int32, (1, LANES), 1)
    slot = jnp.where(lane < SLOTS, lane, jnp.where(lane < 2 * SLOTS, lane - SLOTS, lane - 2 * SLOTS))
    copies[0].wait()
    listed = jnp.concatenate([sites_ref[...], jnp.zeros((1, LANES - SLOTS), jnp.int32)], axis=1)
    site = listed + pltpu.roll(listed, SLOTS, 1) + pltpu.roll(listed, 2 * SLOTS, 1)
    z = site & (LZ - 1)
    y = (site >> 4) & (LY - 1)
    base = site - (y << 4) - z
    near = jnp.where(
        lane < SLOTS,
        site + PLANE,
        jnp.where(
            lane < 2 * SLOTS,
            base + (((y + 1) & (LY - 1)) << 4) + z,
            base + (y << 4) + ((z + 1) & (LZ - 1)),
        ),
    )
    used = lane < 3 * SLOTS
    near = jnp.where(used, near, -1)
    at = jnp.where(used, site, -1)
    marks_ref[0:1, :] = near - SITES
    marks_ref[1:2, :] = slot
    table_copy.wait()
    pairs = jnp.concatenate([table_ref[...], jnp.zeros((1, LANES - ROWS), jnp.int32)], axis=1)
    for g in range(FAR):
        tables_ref[g] = jnp.broadcast_to(pairs, (16, LANES))
    row = lax.broadcasted_iota(jnp.int32, (SITES, LANES), 0)
    pick = jnp.where(row == near, 1.0, 0.0).astype(jnp.bfloat16)
    pick_site = jnp.where(row == at, 1.0, 0.0).astype(jnp.bfloat16)

    rows_ref[...] = jnp.zeros_like(rows_ref)
    copies[1].wait()
    for k in range(3):
        rows_ref[24 * k : 24 * k + 18, :] = links_ref[k]
    exact = rows_ref[...]
    high = exact.astype(jnp.bfloat16).astype(jnp.float32)
    rest = exact - high
    middle = rest.astype(jnp.bfloat16).astype(jnp.float32)
    low = rest - middle
    split = jnp.concatenate([high, middle, low], axis=0).astype(jnp.bfloat16)
    found = jnp.dot(split, pick_site, preferred_element_type=jnp.float32)
    found = found[0:72] + found[72:144] + found[144:216]
    link_ref[...] = jnp.where(
        lane < SLOTS, found[0:24], jnp.where(lane < 2 * SLOTS, found[24:48], found[48:72])
    )
    for c in range(6):
        copies[2 + c].wait()
    plane_ref[...] = modes_ref[:, :, 0:PLANE]
    field = modes_ref[...].reshape(6 * MODES, SITES)
    vec_ref[...] = jnp.dot(field, pick, preferred_element_type=jnp.float32)


def build_local(pair_table, sites, modes, links):
    vmem = pl.BlockSpec(memory_space=pltpu.VMEM)
    hbm = pl.BlockSpec(memory_space=pltpu.HBM)
    return pl.pallas_call(
        local_kernel,
        out_shape=(
            pltpu.VMEM((6, MODES, PLANE), jnp.bfloat16),
            pltpu.VMEM((FAR, 16, LANES), jnp.int32),
            pltpu.VMEM((6 * MODES, LANES), jnp.float32),
            pltpu.VMEM((24, LANES), jnp.float32),
            pltpu.VMEM((8, LANES), jnp.int32),
        ),
        in_specs=[hbm] * 4,
        out_specs=(vmem,) * 5,
        scratch_shapes=[
            pltpu.VMEM((1, ROWS), jnp.int32),
            pltpu.VMEM((1, SLOTS), jnp.int32),
            pltpu.VMEM((6, MODES, SITES), jnp.bfloat16),
            pltpu.VMEM((3, 18, SITES), jnp.float32),
            pltpu.VMEM((72, SITES), jnp.float32),
            pltpu.SemaphoreType.DMA((9,)),
        ],
        compiler_params=pltpu.CompilerParams(vmem_limit_bytes=16 << 20),
        name="local_vectors",
    )(pinned(pair_table.reshape(1, ROWS)), pinned(sites.reshape(1, SLOTS)), pinned(modes), pinned(links))


def build_kernel(counts_ref, vec_ref, link_ref, marks_ref, ahead_ref, out_ref):
    row = lax.broadcasted_iota(jnp.int32, (PLANE, LANES), 0)
    pick_ahead = jnp.where(row == marks_ref[0:1, :], 1.0, 0.0).astype(jnp.bfloat16)
    ahead = ahead_ref[...].reshape(6 * MODES, PLANE)
    vec = vec_ref[...] + jnp.dot(ahead, pick_ahead, preferred_element_type=jnp.float32)
    live = marks_ref[1:2, :] < counts_ref[0]
    link = link_ref[...]
    blank = jnp.zeros((LANES - MODES, LANES), jnp.float32)
    turned = []
    for i in range(3):
        real_part = jnp.zeros((MODES, LANES), jnp.float32)
        imag_part = jnp.zeros((MODES, LANES), jnp.float32)
        for j in range(3):
            at_ij = (i * 3 + j) * 2
            link_re = link[at_ij : at_ij + 1]
            link_im = link[at_ij + 1 : at_ij + 2]
            vec_re = vec[2 * j * MODES : (2 * j + 1) * MODES]
            vec_im = vec[(2 * j + 1) * MODES : (2 * j + 2) * MODES]
            real_part = real_part + link_re * vec_re - link_im * vec_im
            imag_part = imag_part + link_re * vec_im + link_im * vec_re
        for part in (real_part, imag_part):
            turned.append(jnp.concatenate([jnp.where(live, part, 0.0), blank], axis=0).T)
    panel = [turned[c][k * SLOTS : (k + 1) * SLOTS] for k in range(3) for c in range(6)]
    main = jnp.concatenate(panel[:14], axis=0)
    tail = jnp.concatenate(panel[14:], axis=0)
    spread = jnp.concatenate(
        [pltpu.roll(tail, 96, 1), pltpu.roll(tail, 64, 1), pltpu.roll(tail, 32, 1),
         jnp.zeros((WIRE - 288, LANES), jnp.float32)],
        axis=0,
    )
    lane = lax.broadcasted_iota(jnp.int32, (1, LANES), 1)
    out_ref[...] = jnp.where(lane < MODES, main, spread).astype(jnp.bfloat16)


def build(counts, vec, link, marks, ahead):
    vmem = pl.BlockSpec(memory_space=pltpu.VMEM)
    return pl.pallas_call(
        build_kernel,
        out_shape=jax.ShapeDtypeStruct((WIRE, LANES), jnp.bfloat16),
        in_specs=[pl.BlockSpec(memory_space=pltpu.SMEM)] + [vmem] * 4,
        out_specs=vmem,
        compiler_params=pltpu.CompilerParams(vmem_limit_bytes=16 << 20),
        name="build_panel",
    )(counts, vec, link, marks, ahead)


TILES = ((0, 256), (256, 256), (512, 256), (768, 256), (1024, 128))
SHARED = NEAR * SLOTS
STACK = 6 * SHARED


def contract_kernel(*refs):
    panel_refs = refs[:NEAR]
    table_ref, out_ref, side_ref, third_ref, *scratch = refs[NEAR:]
    pick_refs, cross_refs = scratch[:4], scratch[4:]
    lane = lax.broadcasted_iota(jnp.int32, (1, LANES), 1)

    rows = [table_ref[g][0:1] for g in range(FAR)]
    pieces = [
        jnp.where(lane < 64, rows[2 * v], pltpu.roll(rows[2 * v + 1], 64, 1)) for v in range(FAR // 2)
    ]
    last = jnp.zeros((1, LANES), jnp.int32)
    for g in range(FAR):
        moved = pltpu.roll(rows[g], (8 * g - 64) % LANES, 1) if g != 8 else rows[g]
        last = jnp.where((lane >= 8 * g) & (lane < 8 * g + 8), moved, last)
    pairs = jnp.concatenate(pieces + [last], axis=1)
    first = (pairs * 43691) >> 22
    second = pairs - first * MODES

    comps = [[] for _ in range(18)]
    for ref in panel_refs:
        wide = ref[...].astype(jnp.float32)
        for n in range(14):
            comps[n].append(wide[n * SLOTS : (n + 1) * SLOTS])
        tail = jnp.where(
            lane < 32,
            pltpu.roll(wide[0:96], 32, 1),
            jnp.where(lane < 64, pltpu.roll(wide[96:192], 64, 1), pltpu.roll(wide[192:288], 96, 1)),
        )
        for n in range(4):
            comps[14 + n].append(tail[n * SLOTS : (n + 1) * SLOTS])
    comps = [jnp.concatenate(c, axis=0) for c in comps]
    for n in range(12):
        side_ref[n // 6, (n % 6) * SHARED : (n % 6 + 1) * SHARED, :] = comps[n].astype(jnp.bfloat16)

    def third():
        upper = []
        lower = []
        for k in range(3):
            t_re, t_im = comps[12 + 2 * k], comps[13 + 2 * k]
            upper += [t_re, -t_im]
            lower += [t_im, t_re]
        third_ref[0:MODES, :] = jnp.concatenate(upper, axis=0).T[0:MODES].astype(jnp.bfloat16)
        third_ref[MODES : 2 * MODES, :] = jnp.concatenate(lower, axis=0).T[0:MODES].astype(jnp.bfloat16)

    half = lane < 64

    def select(t):
        at, width = TILES[t]
        mode = lax.broadcasted_iota(jnp.int32, (LANES, width), 0)
        for n, index in enumerate((first, second)):
            hot = jnp.where(mode == index[:, at : at + width], 1.0, 0.0).astype(jnp.bfloat16)
            pick_refs[2 * (t % 2) + n][:, 0:width] = jnp.dot(
                side_ref[n], hot, preferred_element_type=jnp.float32
            )

    def cross(t):
        at, width = TILES[t]
        lefts, rights, target = pick_refs[2 * (t % 2)], pick_refs[2 * (t % 2) + 1], cross_refs[t % 2]

        def chunk(q):
            left = [lefts[pl.ds(c * SHARED + q, 16), 0:width] for c in range(6)]
            right = [rights[pl.ds(c * SHARED + q, 16), 0:width] for c in range(6)]

            def cmul(i, j):
                return (
                    left[2 * i] * right[2 * j] - left[2 * i + 1] * right[2 * j + 1],
                    left[2 * i] * right[2 * j + 1] + left[2 * i + 1] * right[2 * j],
                )

            for k, (i, j) in enumerate(((1, 2), (2, 0), (0, 1))):
                plus = cmul(i, j)
                minus = cmul(j, i)
                for r in range(2):
                    target[pl.ds((2 * k + r) * SHARED + q, 16), 0:width] = (plus[r] - minus[r]).astype(
                        jnp.bfloat16
                    )

        for q in range(0, SHARED, 16):
            chunk(q)

    def finish(t):
        at, width = TILES[t]
        summed = jnp.dot(
            third_ref[...], cross_refs[t % 2][:, 0:width], preferred_element_type=jnp.float32
        )
        if width == LANES:
            flat = jnp.concatenate([summed, jnp.zeros((64, LANES), jnp.float32)], axis=0)
            low, high = flat[0:LANES].T, flat[LANES : 2 * LANES].T
            for g in range(FAR):
                both = [low[8 * g : 8 * g + 8], high[8 * g : 8 * g + 8]]
                out_ref[g, MODES : MODES + 16, :] = jnp.concatenate(both, axis=0).astype(jnp.bfloat16)
            return
        for v in range(2):
            real = summed[0:MODES, v * LANES : (v + 1) * LANES]
            imag = summed[MODES : 2 * MODES, v * LANES : (v + 1) * LANES]
            g = at // 64 + 2 * v
            out_ref[g, 0:MODES, :] = jnp.where(half, real, pltpu.roll(imag, 64, 1)).astype(jnp.bfloat16)
            out_ref[g + 1, 0:MODES, :] = jnp.where(half, pltpu.roll(real, 64, 1), imag).astype(
                jnp.bfloat16
            )

    select(0)
    third()
    for t in range(len(TILES)):
        if t + 1 < len(TILES):
            select(t + 1)
        cross(t)
        finish(t)


def contract(panels, tables):
    vmem = pl.BlockSpec(memory_space=pltpu.VMEM)
    return pl.pallas_call(
        contract_kernel,
        out_shape=jax.ShapeDtypeStruct((FAR, PACKED, LANES), jnp.bfloat16),
        in_specs=[vmem] * (NEAR + 1),
        out_specs=vmem,
        scratch_shapes=[
            pltpu.VMEM((2, STACK, LANES), jnp.bfloat16),
            pltpu.VMEM((2 * MODES, STACK), jnp.bfloat16),
        ]
        + [pltpu.VMEM((STACK, 256), jnp.float32)] * 4
        + [pltpu.VMEM((STACK, 256), jnp.bfloat16)] * 2,
        compiler_params=pltpu.CompilerParams(vmem_limit_bytes=40 << 20),
        name="contract_pairs",
    )(*panels, tables)


def total_kernel(scale, parts_ref, out_ref):
    total = parts_ref[0].astype(jnp.float32)
    for g in range(1, FAR):
        total = total + parts_ref[g].astype(jnp.float32)
    total = total * scale
    lane = lax.broadcasted_iota(jnp.int32, (1, LANES), 1)
    main = jnp.concatenate([total[0:MODES], jnp.zeros((LANES - MODES, LANES), jnp.float32)], axis=0).T
    moved = pltpu.roll(main[64:128], 96, 1)
    out_ref[0:64, 0:LANES] = jnp.where(lane < MODES, main[0:64], moved)
    out_ref[0:64, LANES : 2 * MODES] = moved[:, 0:64]
    out_ref[64:72, 0:LANES] = total[MODES : MODES + 8]
    out_ref[64:72, LANES : 2 * MODES] = total[MODES + 8 : MODES + 16, 0:64]


def add_up(parts):
    vmem = pl.BlockSpec(memory_space=pltpu.VMEM)
    scale = float(1.0 / (NEAR * FAR * SLOTS) ** 0.5)
    return pl.pallas_call(
        lambda *refs: total_kernel(scale, *refs),
        out_shape=jax.ShapeDtypeStruct((ROWS, 2 * MODES), jnp.float32),
        in_specs=[vmem],
        out_specs=vmem,
        compiler_params=pltpu.CompilerParams(vmem_limit_bytes=8 << 20),
        name="add_up",
    )(parts)


def swapped(value, bits):
    count = lax.axis_size("gx")
    return lax.ppermute(value, "gx", [(source, source ^ bits) for source in range(count)])


def shards(modes, links, sites, counts, pair_table):
    count = lax.axis_size("gx")
    pairs = [(source, (source - 1) % count) for source in range(count)]
    plane, tables, vec, link, marks = build_local(pair_table, sites, modes, links)
    ahead = lax.ppermute(plane, "gx", pairs)
    tables = lax.all_to_all(tables, "gx", 0, 0, axis_index_groups=FAR_GROUPS)
    panel = build(counts, vec, link, marks, ahead)
    others = [swapped(panel, bits) for bits in (2, 4, 6)]
    panels = [panel] + others
    panels = panels + [swapped(p, 1) for p in panels]
    parts = contract(panels, tables)
    parts = lax.all_to_all(parts, "gx", 0, 0, axis_index_groups=FAR_GROUPS)
    return add_up(parts)


def solution(mesh):
    placed = (P("ta", None, "gx"), P("ta", None, "gx"), P(("ta", "gx")), P(("ta", "gx")), P("gx"))
    return jax.shard_map(
        shards, mesh=mesh, in_specs=placed, out_specs=P(("ta", "gx"), None), check_vma=False
    )
```

```python
import jax
import jax.numpy as jnp
from jax import lax
from jax.experimental import pallas as pl
from jax.experimental.pallas import tpu as pltpu
from jax.sharding import PartitionSpec as P

MODES = 96
LY = 16
LZ = 16
PLANE = LY * LZ
SITES = 1024
SLOTS = 24
ROWS = 72
NEAR = 8
FAR = 16
LANES = 128
FAR_GROUPS = [[NEAR * j + i for j in range(FAR)] for i in range(NEAR)]
PACKED = 112
WIRE = 336


def pinned(value):
    return pltpu.with_memory_space_constraint(value, pltpu.HBM)


def local_kernel(
    table_hbm, sites_hbm, modes_hbm, links_hbm, plane_ref, tables_ref, vec_ref, link_ref, marks_ref,
    table_ref, spread_ref, sites_ref, modes_ref, links_ref, rows_ref, sems,
):
    copies = [
        pltpu.make_async_copy(sites_hbm, sites_ref, sems.at[0]),
        pltpu.make_async_copy(links_hbm, links_ref, sems.at[1]),
    ] + [pltpu.make_async_copy(modes_hbm.at[c], modes_ref.at[c], sems.at[2 + c]) for c in range(6)]
    table_copy = pltpu.make_async_copy(table_hbm, table_ref, sems.at[8])
    table_copy.start()
    for copy in copies:
        copy.start()
    lane = lax.broadcasted_iota(jnp.int32, (1, LANES), 1)
    slot = jnp.where(lane < SLOTS, lane, jnp.where(lane < 2 * SLOTS, lane - SLOTS, lane - 2 * SLOTS))
    copies[0].wait()
    listed = jnp.concatenate([sites_ref[...], jnp.zeros((1, LANES - SLOTS), jnp.int32)], axis=1)
    site = listed + pltpu.roll(listed, SLOTS, 1) + pltpu.roll(listed, 2 * SLOTS, 1)
    z = site & (LZ - 1)
    y = (site >> 4) & (LY - 1)
    base = site - (y << 4) - z
    near = jnp.where(
        lane < SLOTS,
        site + PLANE,
        jnp.where(
            lane < 2 * SLOTS,
            base + (((y + 1) & (LY - 1)) << 4) + z,
            base + (y << 4) + ((z + 1) & (LZ - 1)),
        ),
    )
    used = lane < 3 * SLOTS
    near = jnp.where(used, near, -1)
    at = jnp.where(used, site, -1)
    marks_ref[0:1, :] = near - SITES
    marks_ref[1:2, :] = slot
    table_copy.wait()
    pairs = jnp.concatenate([table_ref[...], jnp.zeros((1, LANES - ROWS), jnp.int32)], axis=1)
    for g in range(FAR):
        spread_ref[g] = jnp.broadcast_to(pairs, (16, LANES))
    out_copy = pltpu.make_async_copy(spread_ref, tables_ref, sems.at[9])
    out_copy.start()
    row = lax.broadcasted_iota(jnp.int32, (SITES, LANES), 0)
    pick = jnp.where(row == near, 1.0, 0.0).astype(jnp.bfloat16)
    pick_site = jnp.where(row == at, 1.0, 0.0).astype(jnp.bfloat16)

    rows_ref[...] = jnp.zeros_like(rows_ref)
    copies[1].wait()
    for k in range(3):
        rows_ref[24 * k : 24 * k + 18, :] = links_ref[k]
    exact = rows_ref[...]
    high = exact.astype(jnp.bfloat16).astype(jnp.float32)
    rest = exact - high
    middle = rest.astype(jnp.bfloat16).astype(jnp.float32)
    low = rest - middle
    split = jnp.concatenate([high, middle, low], axis=0).astype(jnp.bfloat16)
    found = jnp.dot(split, pick_site, preferred_element_type=jnp.float32)
    found = found[0:72] + found[72:144] + found[144:216]
    link_ref[...] = jnp.where(
        lane < SLOTS, found[0:24], jnp.where(lane < 2 * SLOTS, found[24:48], found[48:72])
    )
    for c in range(6):
        copies[2 + c].wait()
    plane_ref[...] = modes_ref[:, :, 0:PLANE]
    field = modes_ref[...].reshape(6 * MODES, SITES)
    vec_ref[...] = jnp.dot(field, pick, preferred_element_type=jnp.float32)
    out_copy.wait()


def build_local(pair_table, sites, modes, links):
    vmem = pl.BlockSpec(memory_space=pltpu.VMEM)
    hbm = pl.BlockSpec(memory_space=pltpu.HBM)
    return pl.pallas_call(
        local_kernel,
        out_shape=(
            pltpu.VMEM((6, MODES, PLANE), jnp.bfloat16),
            pltpu.HBM((FAR, 16, LANES), jnp.int32),
            pltpu.VMEM((6 * MODES, LANES), jnp.float32),
            pltpu.VMEM((24, LANES), jnp.float32),
            pltpu.VMEM((8, LANES), jnp.int32),
        ),
        in_specs=[hbm] * 4,
        out_specs=(vmem, hbm, vmem, vmem, vmem),
        scratch_shapes=[
            pltpu.VMEM((1, ROWS), jnp.int32),
            pltpu.VMEM((FAR, 16, LANES), jnp.int32),
            pltpu.VMEM((1, SLOTS), jnp.int32),
            pltpu.VMEM((6, MODES, SITES), jnp.bfloat16),
            pltpu.VMEM((3, 18, SITES), jnp.float32),
            pltpu.VMEM((72, SITES), jnp.float32),
            pltpu.SemaphoreType.DMA((10,)),
        ],
        compiler_params=pltpu.CompilerParams(vmem_limit_bytes=16 << 20),
        name="local_vectors",
    )(pinned(pair_table.reshape(1, ROWS)), pinned(sites.reshape(1, SLOTS)), pinned(modes), pinned(links))


def build_kernel(counts_ref, vec_ref, link_ref, marks_ref, ahead_ref, out_ref):
    row = lax.broadcasted_iota(jnp.int32, (PLANE, LANES), 0)
    pick_ahead = jnp.where(row == marks_ref[0:1, :], 1.0, 0.0).astype(jnp.bfloat16)
    ahead = ahead_ref[...].reshape(6 * MODES, PLANE)
    vec = vec_ref[...] + jnp.dot(ahead, pick_ahead, preferred_element_type=jnp.float32)
    live = marks_ref[1:2, :] < counts_ref[0]
    link = link_ref[...]
    blank = jnp.zeros((LANES - MODES, LANES), jnp.float32)
    turned = []
    for i in range(3):
        real_part = jnp.zeros((MODES, LANES), jnp.float32)
        imag_part = jnp.zeros((MODES, LANES), jnp.float32)
        for j in range(3):
            at_ij = (i * 3 + j) * 2
            link_re = link[at_ij : at_ij + 1]
            link_im = link[at_ij + 1 : at_ij + 2]
            vec_re = vec[2 * j * MODES : (2 * j + 1) * MODES]
            vec_im = vec[(2 * j + 1) * MODES : (2 * j + 2) * MODES]
            real_part = real_part + link_re * vec_re - link_im * vec_im
            imag_part = imag_part + link_re * vec_im + link_im * vec_re
        for part in (real_part, imag_part):
            turned.append(jnp.concatenate([jnp.where(live, part, 0.0), blank], axis=0).T)
    panel = [turned[c][k * SLOTS : (k + 1) * SLOTS] for k in range(3) for c in range(6)]
    main = jnp.concatenate(panel[:14], axis=0)
    tail = jnp.concatenate(panel[14:], axis=0)
    spread = jnp.concatenate(
        [pltpu.roll(tail, 96, 1), pltpu.roll(tail, 64, 1), pltpu.roll(tail, 32, 1),
         jnp.zeros((WIRE - 288, LANES), jnp.float32)],
        axis=0,
    )
    lane = lax.broadcasted_iota(jnp.int32, (1, LANES), 1)
    out_ref[...] = jnp.where(lane < MODES, main, spread).astype(jnp.bfloat16)


def build(counts, vec, link, marks, ahead):
    vmem = pl.BlockSpec(memory_space=pltpu.VMEM)
    return pl.pallas_call(
        build_kernel,
        out_shape=jax.ShapeDtypeStruct((WIRE, LANES), jnp.bfloat16),
        in_specs=[pl.BlockSpec(memory_space=pltpu.SMEM)] + [vmem] * 4,
        out_specs=vmem,
        compiler_params=pltpu.CompilerParams(vmem_limit_bytes=16 << 20),
        name="build_panel",
    )(counts, vec, link, marks, ahead)


TILES = ((0, 256), (256, 256), (512, 256), (768, 256), (1024, 128))
SHARED = NEAR * SLOTS
STACK = 6 * SHARED


def contract_kernel(*refs):
    panel_refs = refs[:NEAR]
    table_ref, out_ref, side_ref, third_ref, *scratch = refs[NEAR:]
    pick_refs, cross_refs = scratch[:4], scratch[4:]
    lane = lax.broadcasted_iota(jnp.int32, (1, LANES), 1)

    rows = [table_ref[g][0:1] for g in range(FAR)]
    pieces = [
        jnp.where(lane < 64, rows[2 * v], pltpu.roll(rows[2 * v + 1], 64, 1)) for v in range(FAR // 2)
    ]
    last = jnp.zeros((1, LANES), jnp.int32)
    for g in range(FAR):
        moved = pltpu.roll(rows[g], (8 * g - 64) % LANES, 1) if g != 8 else rows[g]
        last = jnp.where((lane >= 8 * g) & (lane < 8 * g + 8), moved, last)
    pairs = jnp.concatenate(pieces + [last], axis=1)
    first = (pairs * 43691) >> 22
    second = pairs - first * MODES

    comps = [[] for _ in range(18)]
    for ref in panel_refs:
        wide = ref[...].astype(jnp.float32)
        for n in range(14):
            comps[n].append(wide[n * SLOTS : (n + 1) * SLOTS])
        tail = jnp.where(
            lane < 32,
            pltpu.roll(wide[0:96], 32, 1),
            jnp.where(lane < 64, pltpu.roll(wide[96:192], 64, 1), pltpu.roll(wide[192:288], 96, 1)),
        )
        for n in range(4):
            comps[14 + n].append(tail[n * SLOTS : (n + 1) * SLOTS])
    comps = [jnp.concatenate(c, axis=0) for c in comps]
    for n in range(12):
        side_ref[n // 6, (n % 6) * SHARED : (n % 6 + 1) * SHARED, :] = comps[n].astype(jnp.bfloat16)

    def third():
        upper = []
        lower = []
        for k in range(3):
            t_re, t_im = comps[12 + 2 * k], comps[13 + 2 * k]
            upper += [t_re, -t_im]
            lower += [t_im, t_re]
        third_ref[0:MODES, :] = jnp.concatenate(upper, axis=0).T[0:MODES].astype(jnp.bfloat16)
        third_ref[MODES : 2 * MODES, :] = jnp.concatenate(lower, axis=0).T[0:MODES].astype(jnp.bfloat16)

    half = lane < 64

    def select(t):
        at, width = TILES[t]
        mode = lax.broadcasted_iota(jnp.int32, (LANES, width), 0)
        for n, index in enumerate((first, second)):
            hot = jnp.where(mode == index[:, at : at + width], 1.0, 0.0).astype(jnp.bfloat16)
            pick_refs[2 * (t % 2) + n][:, 0:width] = jnp.dot(
                side_ref[n], hot, preferred_element_type=jnp.float32
            )

    def cross(t):
        at, width = TILES[t]
        lefts, rights, target = pick_refs[2 * (t % 2)], pick_refs[2 * (t % 2) + 1], cross_refs[t % 2]

        def chunk(q):
            left = [lefts[pl.ds(c * SHARED + q, 16), 0:width] for c in range(6)]
            right = [rights[pl.ds(c * SHARED + q, 16), 0:width] for c in range(6)]

            def cmul(i, j):
                return (
                    left[2 * i] * right[2 * j] - left[2 * i + 1] * right[2 * j + 1],
                    left[2 * i] * right[2 * j + 1] + left[2 * i + 1] * right[2 * j],
                )

            for k, (i, j) in enumerate(((1, 2), (2, 0), (0, 1))):
                plus = cmul(i, j)
                minus = cmul(j, i)
                for r in range(2):
                    target[pl.ds((2 * k + r) * SHARED + q, 16), 0:width] = (plus[r] - minus[r]).astype(
                        jnp.bfloat16
                    )

        for q in range(0, SHARED, 16):
            chunk(q)

    def finish(t):
        at, width = TILES[t]
        summed = jnp.dot(
            third_ref[...], cross_refs[t % 2][:, 0:width], preferred_element_type=jnp.float32
        )
        if width == LANES:
            flat = jnp.concatenate([summed, jnp.zeros((64, LANES), jnp.float32)], axis=0)
            low, high = flat[0:LANES].T, flat[LANES : 2 * LANES].T
            for g in range(FAR):
                both = [low[8 * g : 8 * g + 8], high[8 * g : 8 * g + 8]]
                out_ref[g, MODES : MODES + 16, :] = jnp.concatenate(both, axis=0).astype(jnp.bfloat16)
            return
        for v in range(2):
            real = summed[0:MODES, v * LANES : (v + 1) * LANES]
            imag = summed[MODES : 2 * MODES, v * LANES : (v + 1) * LANES]
            g = at // 64 + 2 * v
            out_ref[g, 0:MODES, :] = jnp.where(half, real, pltpu.roll(imag, 64, 1)).astype(jnp.bfloat16)
            out_ref[g + 1, 0:MODES, :] = jnp.where(half, pltpu.roll(real, 64, 1), imag).astype(
                jnp.bfloat16
            )

    select(0)
    third()
    for t in range(len(TILES)):
        if t + 1 < len(TILES):
            select(t + 1)
        cross(t)
        finish(t)


def contract(panels, tables):
    vmem = pl.BlockSpec(memory_space=pltpu.VMEM)
    return pl.pallas_call(
        contract_kernel,
        out_shape=jax.ShapeDtypeStruct((FAR, PACKED, LANES), jnp.bfloat16),
        in_specs=[vmem] * (NEAR + 1),
        out_specs=vmem,
        scratch_shapes=[
            pltpu.VMEM((2, STACK, LANES), jnp.bfloat16),
            pltpu.VMEM((2 * MODES, STACK), jnp.bfloat16),
        ]
        + [pltpu.VMEM((STACK, 256), jnp.float32)] * 4
        + [pltpu.VMEM((STACK, 256), jnp.bfloat16)] * 2,
        compiler_params=pltpu.CompilerParams(vmem_limit_bytes=40 << 20),
        name="contract_pairs",
    )(*panels, tables)


def total_kernel(scale, parts_ref, out_ref):
    total = parts_ref[0].astype(jnp.float32)
    for g in range(1, FAR):
        total = total + parts_ref[g].astype(jnp.float32)
    total = total * scale
    lane = lax.broadcasted_iota(jnp.int32, (1, LANES), 1)
    main = jnp.concatenate([total[0:MODES], jnp.zeros((LANES - MODES, LANES), jnp.float32)], axis=0).T
    moved = pltpu.roll(main[64:128], 96, 1)
    out_ref[0:64, 0:LANES] = jnp.where(lane < MODES, main[0:64], moved)
    out_ref[0:64, LANES : 2 * MODES] = moved[:, 0:64]
    out_ref[64:72, 0:LANES] = total[MODES : MODES + 8]
    out_ref[64:72, LANES : 2 * MODES] = total[MODES + 8 : MODES + 16, 0:64]


def add_up(parts):
    vmem = pl.BlockSpec(memory_space=pltpu.VMEM)
    scale = float(1.0 / (NEAR * FAR * SLOTS) ** 0.5)
    return pl.pallas_call(
        lambda *refs: total_kernel(scale, *refs),
        out_shape=jax.ShapeDtypeStruct((ROWS, 2 * MODES), jnp.float32),
        in_specs=[vmem],
        out_specs=vmem,
        compiler_params=pltpu.CompilerParams(vmem_limit_bytes=8 << 20),
        name="add_up",
    )(parts)


def swapped(value, bits):
    count = lax.axis_size("gx")
    return lax.ppermute(value, "gx", [(source, source ^ bits) for source in range(count)])


def shards(modes, links, sites, counts, pair_table):
    count = lax.axis_size("gx")
    pairs = [(source, (source - 1) % count) for source in range(count)]
    plane, tables, vec, link, marks = build_local(pair_table, sites, modes, links)
    ahead = lax.ppermute(plane, "gx", pairs)
    tables = lax.all_to_all(tables, "gx", 0, 0, axis_index_groups=FAR_GROUPS)
    panel = build(counts, vec, link, marks, ahead)
    others = [swapped(panel, bits) for bits in (2, 4, 6)]
    panels = [panel] + others
    panels = panels + [swapped(p, 1) for p in panels]
    parts = contract(panels, tables)
    parts = lax.all_to_all(parts, "gx", 0, 0, axis_index_groups=FAR_GROUPS)
    return add_up(parts)


def solution(mesh):
    placed = (P("ta", None, "gx"), P("ta", None, "gx"), P(("ta", "gx")), P(("ta", "gx")), P("gx"))
    return jax.shard_map(
        shards, mesh=mesh, in_specs=placed, out_specs=P(("ta", "gx"), None), check_vma=False
    )
```

```python
import jax
import jax.numpy as jnp
from jax import lax
from jax.experimental import pallas as pl
from jax.experimental.pallas import tpu as pltpu
from jax.sharding import PartitionSpec as P

MODES = 96
LY = 16
LZ = 16
PLANE = LY * LZ
SITES = 1024
SLOTS = 24
ROWS = 72
NEAR = 8
FAR = 16
LANES = 128
FAR_GROUPS = [[i ^ j for j in [0, 2, 4, 6, 8, 10, 12, 14, 64, 66, 68, 70, 72, 74, 76, 78]] for i in [0, 1, 16, 17, 32, 33, 48, 49]]
PACKED = 112
WIRE = 336


def pinned(value):
    return pltpu.with_memory_space_constraint(value, pltpu.HBM)


def local_kernel(
    table_hbm, sites_hbm, modes_hbm, links_hbm, plane_ref, tables_ref, vec_ref, link_ref, marks_ref,
    table_ref, spread_ref, sites_ref, modes_ref, links_ref, rows_ref, sems,
):
    copies = [
        pltpu.make_async_copy(sites_hbm, sites_ref, sems.at[0]),
        pltpu.make_async_copy(links_hbm, links_ref, sems.at[1]),
    ] + [pltpu.make_async_copy(modes_hbm.at[c], modes_ref.at[c], sems.at[2 + c]) for c in range(6)]
    table_copy = pltpu.make_async_copy(table_hbm, table_ref, sems.at[8])
    table_copy.start()
    for copy in copies:
        copy.start()
    lane = lax.broadcasted_iota(jnp.int32, (1, LANES), 1)
    slot = jnp.where(lane < SLOTS, lane, jnp.where(lane < 2 * SLOTS, lane - SLOTS, lane - 2 * SLOTS))
    copies[0].wait()
    listed = jnp.concatenate([sites_ref[...], jnp.zeros((1, LANES - SLOTS), jnp.int32)], axis=1)
    site = listed + pltpu.roll(listed, SLOTS, 1) + pltpu.roll(listed, 2 * SLOTS, 1)
    z = site & (LZ - 1)
    y = (site >> 4) & (LY - 1)
    base = site - (y << 4) - z
    near = jnp.where(
        lane < SLOTS,
        site + PLANE,
        jnp.where(
            lane < 2 * SLOTS,
            base + (((y + 1) & (LY - 1)) << 4) + z,
            base + (y << 4) + ((z + 1) & (LZ - 1)),
        ),
    )
    used = lane < 3 * SLOTS
    near = jnp.where(used, near, -1)
    at = jnp.where(used, site, -1)
    marks_ref[0:1, :] = near - SITES
    marks_ref[1:2, :] = slot
    table_copy.wait()
    pairs = jnp.concatenate([table_ref[...], jnp.zeros((1, LANES - ROWS), jnp.int32)], axis=1)
    for g in range(FAR):
        spread_ref[g] = jnp.broadcast_to(pairs, (16, LANES))
    out_copy = pltpu.make_async_copy(spread_ref, tables_ref, sems.at[9])
    out_copy.start()
    row = lax.broadcasted_iota(jnp.int32, (SITES, LANES), 0)
    pick = jnp.where(row == near, 1.0, 0.0).astype(jnp.bfloat16)
    pick_site = jnp.where(row == at, 1.0, 0.0).astype(jnp.bfloat16)

    rows_ref[...] = jnp.zeros_like(rows_ref)
    copies[1].wait()
    for k in range(3):
        rows_ref[24 * k : 24 * k + 18, :] = links_ref[k]
    exact = rows_ref[...]
    high = exact.astype(jnp.bfloat16).astype(jnp.float32)
    rest = exact - high
    middle = rest.astype(jnp.bfloat16).astype(jnp.float32)
    low = rest - middle
    split = jnp.concatenate([high, middle, low], axis=0).astype(jnp.bfloat16)
    found = jnp.dot(split, pick_site, preferred_element_type=jnp.float32)
    found = found[0:72] + found[72:144] + found[144:216]
    link_ref[...] = jnp.where(
        lane < SLOTS, found[0:24], jnp.where(lane < 2 * SLOTS, found[24:48], found[48:72])
    )
    for c in range(6):
        copies[2 + c].wait()
    plane_ref[...] = modes_ref[:, :, 0:PLANE]
    field = modes_ref[...].reshape(6 * MODES, SITES)
    vec_ref[...] = jnp.dot(field, pick, preferred_element_type=jnp.float32)
    out_copy.wait()


def build_local(pair_table, sites, modes, links):
    vmem = pl.BlockSpec(memory_space=pltpu.VMEM)
    hbm = pl.BlockSpec(memory_space=pltpu.HBM)
    return pl.pallas_call(
        local_kernel,
        out_shape=(
            pltpu.VMEM((6, MODES, PLANE), jnp.bfloat16),
            pltpu.HBM((FAR, 16, LANES), jnp.int32),
            pltpu.VMEM((6 * MODES, LANES), jnp.float32),
            pltpu.VMEM((24, LANES), jnp.float32),
            pltpu.VMEM((8, LANES), jnp.int32),
        ),
        in_specs=[hbm] * 4,
        out_specs=(vmem, hbm, vmem, vmem, vmem),
        scratch_shapes=[
            pltpu.VMEM((1, ROWS), jnp.int32),
            pltpu.VMEM((FAR, 16, LANES), jnp.int32),
            pltpu.VMEM((1, SLOTS), jnp.int32),
            pltpu.VMEM((6, MODES, SITES), jnp.bfloat16),
            pltpu.VMEM((3, 18, SITES), jnp.float32),
            pltpu.VMEM((72, SITES), jnp.float32),
            pltpu.SemaphoreType.DMA((10,)),
        ],
        compiler_params=pltpu.CompilerParams(vmem_limit_bytes=16 << 20),
        name="local_vectors",
    )(pinned(pair_table.reshape(1, ROWS)), pinned(sites.reshape(1, SLOTS)), pinned(modes), pinned(links))


def build_kernel(counts_ref, vec_ref, link_ref, marks_ref, ahead_ref, out_ref):
    row = lax.broadcasted_iota(jnp.int32, (PLANE, LANES), 0)
    pick_ahead = jnp.where(row == marks_ref[0:1, :], 1.0, 0.0).astype(jnp.bfloat16)
    ahead = ahead_ref[...].reshape(6 * MODES, PLANE)
    vec = vec_ref[...] + jnp.dot(ahead, pick_ahead, preferred_element_type=jnp.float32)
    live = marks_ref[1:2, :] < counts_ref[0]
    link = link_ref[...]
    blank = jnp.zeros((LANES - MODES, LANES), jnp.float32)
    turned = []
    for i in range(3):
        real_part = jnp.zeros((MODES, LANES), jnp.float32)
        imag_part = jnp.zeros((MODES, LANES), jnp.float32)
        for j in range(3):
            at_ij = (i * 3 + j) * 2
            link_re = link[at_ij : at_ij + 1]
            link_im = link[at_ij + 1 : at_ij + 2]
            vec_re = vec[2 * j * MODES : (2 * j + 1) * MODES]
            vec_im = vec[(2 * j + 1) * MODES : (2 * j + 2) * MODES]
            real_part = real_part + link_re * vec_re - link_im * vec_im
            imag_part = imag_part + link_re * vec_im + link_im * vec_re
        for part in (real_part, imag_part):
            turned.append(jnp.concatenate([jnp.where(live, part, 0.0), blank], axis=0).T)
    panel = [turned[c][k * SLOTS : (k + 1) * SLOTS] for k in range(3) for c in range(6)]
    main = jnp.concatenate(panel[:14], axis=0)
    tail = jnp.concatenate(panel[14:], axis=0)
    spread = jnp.concatenate(
        [pltpu.roll(tail, 96, 1), pltpu.roll(tail, 64, 1), pltpu.roll(tail, 32, 1),
         jnp.zeros((WIRE - 288, LANES), jnp.float32)],
        axis=0,
    )
    lane = lax.broadcasted_iota(jnp.int32, (1, LANES), 1)
    out_ref[...] = jnp.where(lane < MODES, main, spread).astype(jnp.bfloat16)


def build(counts, vec, link, marks, ahead):
    vmem = pl.BlockSpec(memory_space=pltpu.VMEM)
    return pl.pallas_call(
        build_kernel,
        out_shape=jax.ShapeDtypeStruct((WIRE, LANES), jnp.bfloat16),
        in_specs=[pl.BlockSpec(memory_space=pltpu.SMEM)] + [vmem] * 4,
        out_specs=vmem,
        compiler_params=pltpu.CompilerParams(vmem_limit_bytes=16 << 20),
        name="build_panel",
    )(counts, vec, link, marks, ahead)


TILES = ((0, 256), (256, 256), (512, 256), (768, 256), (1024, 128))
SHARED = NEAR * SLOTS
STACK = 6 * SHARED


def contract_kernel(*refs):
    panel_refs = refs[:NEAR]
    table_ref, out_ref, side_ref, third_ref, *scratch = refs[NEAR:]
    pick_refs, cross_refs = scratch[:4], scratch[4:]
    lane = lax.broadcasted_iota(jnp.int32, (1, LANES), 1)

    rows = [table_ref[g][0:1] for g in range(FAR)]
    pieces = [
        jnp.where(lane < 64, rows[2 * v], pltpu.roll(rows[2 * v + 1], 64, 1)) for v in range(FAR // 2)
    ]
    last = jnp.zeros((1, LANES), jnp.int32)
    for g in range(FAR):
        moved = pltpu.roll(rows[g], (8 * g - 64) % LANES, 1) if g != 8 else rows[g]
        last = jnp.where((lane >= 8 * g) & (lane < 8 * g + 8), moved, last)
    pairs = jnp.concatenate(pieces + [last], axis=1)
    first = (pairs * 43691) >> 22
    second = pairs - first * MODES

    comps = [[] for _ in range(18)]
    for ref in panel_refs:
        wide = ref[...].astype(jnp.float32)
        for n in range(14):
            comps[n].append(wide[n * SLOTS : (n + 1) * SLOTS])
        tail = jnp.where(
            lane < 32,
            pltpu.roll(wide[0:96], 32, 1),
            jnp.where(lane < 64, pltpu.roll(wide[96:192], 64, 1), pltpu.roll(wide[192:288], 96, 1)),
        )
        for n in range(4):
            comps[14 + n].append(tail[n * SLOTS : (n + 1) * SLOTS])
    comps = [jnp.concatenate(c, axis=0) for c in comps]
    for n in range(12):
        side_ref[n // 6, (n % 6) * SHARED : (n % 6 + 1) * SHARED, :] = comps[n].astype(jnp.bfloat16)

    def third():
        upper = []
        lower = []
        for k in range(3):
            t_re, t_im = comps[12 + 2 * k], comps[13 + 2 * k]
            upper += [t_re, -t_im]
            lower += [t_im, t_re]
        third_ref[0:MODES, :] = jnp.concatenate(upper, axis=0).T[0:MODES].astype(jnp.bfloat16)
        third_ref[MODES : 2 * MODES, :] = jnp.concatenate(lower, axis=0).T[0:MODES].astype(jnp.bfloat16)

    half = lane < 64

    def select(t):
        at, width = TILES[t]
        mode = lax.broadcasted_iota(jnp.int32, (LANES, width), 0)
        for n, index in enumerate((first, second)):
            hot = jnp.where(mode == index[:, at : at + width], 1.0, 0.0).astype(jnp.bfloat16)
            pick_refs[2 * (t % 2) + n][:, 0:width] = jnp.dot(
                side_ref[n], hot, preferred_element_type=jnp.float32
            )

    def cross(t):
        at, width = TILES[t]
        lefts, rights, target = pick_refs[2 * (t % 2)], pick_refs[2 * (t % 2) + 1], cross_refs[t % 2]

        def chunk(q):
            left = [lefts[pl.ds(c * SHARED + q, 16), 0:width] for c in range(6)]
            right = [rights[pl.ds(c * SHARED + q, 16), 0:width] for c in range(6)]

            def cmul(i, j):
                return (
                    left[2 * i] * right[2 * j] - left[2 * i + 1] * right[2 * j + 1],
                    left[2 * i] * right[2 * j + 1] + left[2 * i + 1] * right[2 * j],
                )

            for k, (i, j) in enumerate(((1, 2), (2, 0), (0, 1))):
                plus = cmul(i, j)
                minus = cmul(j, i)
                for r in range(2):
                    target[pl.ds((2 * k + r) * SHARED + q, 16), 0:width] = (plus[r] - minus[r]).astype(
                        jnp.bfloat16
                    )

        for q in range(0, SHARED, 16):
            chunk(q)

    def finish(t):
        at, width = TILES[t]
        summed = jnp.dot(
            third_ref[...], cross_refs[t % 2][:, 0:width], preferred_element_type=jnp.float32
        )
        if width == LANES:
            flat = jnp.concatenate([summed, jnp.zeros((64, LANES), jnp.float32)], axis=0)
            low, high = flat[0:LANES].T, flat[LANES : 2 * LANES].T
            for g in range(FAR):
                both = [low[8 * g : 8 * g + 8], high[8 * g : 8 * g + 8]]
                out_ref[g, MODES : MODES + 16, :] = jnp.concatenate(both, axis=0).astype(jnp.bfloat16)
            return
        for v in range(2):
            real = summed[0:MODES, v * LANES : (v + 1) * LANES]
            imag = summed[MODES : 2 * MODES, v * LANES : (v + 1) * LANES]
            g = at // 64 + 2 * v
            out_ref[g, 0:MODES, :] = jnp.where(half, real, pltpu.roll(imag, 64, 1)).astype(jnp.bfloat16)
            out_ref[g + 1, 0:MODES, :] = jnp.where(half, pltpu.roll(real, 64, 1), imag).astype(
                jnp.bfloat16
            )

    select(0)
    third()
    for t in range(len(TILES)):
        if t + 1 < len(TILES):
            select(t + 1)
        cross(t)
        finish(t)


def contract(panels, tables):
    vmem = pl.BlockSpec(memory_space=pltpu.VMEM)
    return pl.pallas_call(
        contract_kernel,
        out_shape=jax.ShapeDtypeStruct((FAR, PACKED, LANES), jnp.bfloat16),
        in_specs=[vmem] * (NEAR + 1),
        out_specs=vmem,
        scratch_shapes=[
            pltpu.VMEM((2, STACK, LANES), jnp.bfloat16),
            pltpu.VMEM((2 * MODES, STACK), jnp.bfloat16),
        ]
        + [pltpu.VMEM((STACK, 256), jnp.float32)] * 4
        + [pltpu.VMEM((STACK, 256), jnp.bfloat16)] * 2,
        compiler_params=pltpu.CompilerParams(vmem_limit_bytes=40 << 20),
        name="contract_pairs",
    )(*panels, tables)


def total_kernel(scale, parts_ref, out_ref):
    total = parts_ref[0].astype(jnp.float32)
    for g in range(1, FAR):
        total = total + parts_ref[g].astype(jnp.float32)
    total = total * scale
    lane = lax.broadcasted_iota(jnp.int32, (1, LANES), 1)
    main = jnp.concatenate([total[0:MODES], jnp.zeros((LANES - MODES, LANES), jnp.float32)], axis=0).T
    moved = pltpu.roll(main[64:128], 96, 1)
    out_ref[0:64, 0:LANES] = jnp.where(lane < MODES, main[0:64], moved)
    out_ref[0:64, LANES : 2 * MODES] = moved[:, 0:64]
    out_ref[64:72, 0:LANES] = total[MODES : MODES + 8]
    out_ref[64:72, LANES : 2 * MODES] = total[MODES + 8 : MODES + 16, 0:64]


def add_up(parts):
    vmem = pl.BlockSpec(memory_space=pltpu.VMEM)
    scale = float(1.0 / (NEAR * FAR * SLOTS) ** 0.5)
    return pl.pallas_call(
        lambda *refs: total_kernel(scale, *refs),
        out_shape=jax.ShapeDtypeStruct((ROWS, 2 * MODES), jnp.float32),
        in_specs=[vmem],
        out_specs=vmem,
        compiler_params=pltpu.CompilerParams(vmem_limit_bytes=8 << 20),
        name="add_up",
    )(parts)


def swapped(value, bits):
    count = lax.axis_size("gx")
    return lax.ppermute(value, "gx", [(source, source ^ bits) for source in range(count)])


def shards(modes, links, sites, counts, pair_table):
    count = lax.axis_size("gx")
    pairs = [(source, (source - 1) % count) for source in range(count)]
    plane, tables, vec, link, marks = build_local(pair_table, sites, modes, links)
    ahead = lax.ppermute(plane, "gx", pairs)
    tables = lax.all_to_all(tables, "gx", 0, 0, axis_index_groups=FAR_GROUPS)
    panel = build(counts, vec, link, marks, ahead)
    others = [swapped(panel, bits) for bits in (16, 48, 32)]
    panels = [panel] + others
    panels = panels + [swapped(p, 1) for p in panels]
    parts = contract(panels, tables)
    parts = lax.all_to_all(parts, "gx", 0, 0, axis_index_groups=FAR_GROUPS)
    return add_up(parts)


def solution(mesh):
    placed = (P("ta", None, "gx"), P("ta", None, "gx"), P(("ta", "gx")), P(("ta", "gx")), P("gx"))
    return jax.shard_map(
        shards, mesh=mesh, in_specs=placed, out_specs=P(("ta", "gx"), None), check_vma=False
    )
```
